128 devices in a mesh: section: 8 (over x, core), tp: 16 (over z, y).
Axes of the slice: x: 4, y: 4, z: 4, core: 2. Of those that a mesh axis runs over, the one named last changes fastest.
Arguments:
- tokens: bfloat16 [1024, 4096], P('section', 'tp'), may hold values from -6 to 6
- norm_gain: float32 [4096], replicated, may hold values from 0.5 to 1.5
- in_x: bfloat16 [4096, 16384], P('section', 'tp'), may hold values from -0.09375 to 0.09375
- in_z: bfloat16 [4096, 16384], P('section', 'tp'), may hold values from -0.09375 to 0.09375
- conv_weight: float32 [4, 16384], P(None, 'tp'), may hold values from -3 to 3
- conv_bias: float32 [16384], P('tp'), may hold values from -0.5 to 0.5
- xproj_weight: bfloat16 [16384, 544], P('tp'), may hold values from -0.046875 to 0.046875
- dt_weight: bfloat16 [512, 16384], P(None, 'tp'), may hold values from -0.25 to 0.25
- dt_bias: float32 [16384], P('tp'), may hold values from -6 to -2
- a_log: float32 [16384, 16], P('tp'), may hold values from -2 to 1
- skip_d: float32 [16384], P('tp'), may hold values from 0.5 to 1.5
- out_weight: bfloat16 [16384, 4096], P('tp', 'section'), may hold values from -0.046875 to 0.046875
- moe_gain: float32 [4096], replicated, may hold values from 0.5 to 1.5
- expert_ids: int32 [1024, 2], P('section'), may hold values from 0 to 7, all different within a row; in each aligned block of 128 rows (0 to 127, 128 to 255, ...) at most 48 rows name the same one
- route_gates: float32 [1024, 2], P('section'), may hold values from 0.2 to 1
- w_gate: bfloat16 [8, 4096, 12288], P('section', None, 'tp'), may hold values from -0.09375 to 0.09375
- w_up: bfloat16 [8, 4096, 12288], P('section', None, 'tp'), may hold values from -0.09375 to 0.09375
- w_down: bfloat16 [8, 12288, 4096], P('section', 'tp'), may hold values from -0.0546875 to 0.0546875
Outputs:
- mixed: bfloat16 [1024, 4096], P('section', 'tp')
The draws below stay inside these ranges and needn't reach their ends.
Inputs may be any that keep to these rules, and one draw needn't show every extreme that they name: `expert_ids`: each row names 2 different experts. Within each aligned block of 128 rows (one section block) no expert is named by more than 48 rows, a bound that some block reaches.
All inputs are finite; a program needn't handle non-finite values.
Results may differ from the reference program's by a relative error of at most 0.024.
Values may be sent and summed in bfloat16 or wider, within the bound.
No kernel may reach another device: no remote copies, remote signals or barrier semaphores. Data moves between devices by JAX's collectives and lax.ppermute only.
A program may use at most 192 MiB of HBM per device.

```python
import math
import jax
import jax.numpy as jnp
import numpy as np
from jax import lax

D = 4096
INNER = 16384
STATE = 16
RANK = 512
CONV = 4
FF = 12288
TOPK = 2
BLK = 128
SEQ = 1024
EXPERTS = 8
CAP = 48
N_SECTION = 8
N_TP = 16


def level_of(rng, extent, cuts, low, largest):
    level, own = 1.0, jax.random.fold_in(rng, 6)
    for axis_at, shards_of in cuts:
        heights = jnp.exp(jax.random.uniform(jax.random.fold_in(own, axis_at), (shards_of,), jnp.float32, low / len(cuts), largest / len(cuts)))
        level = level * jnp.repeat(heights, extent[axis_at] // shards_of).reshape([-1 if axis == axis_at else 1 for axis in range(len(extent))])
    return level


def assign_block(own_key, own, number, rows, count, top, most, lean):
    sequence = jax.random.permutation(own_key, count)
    heavy_load, common = load_shares(count, rows * top, most, lean, True), load_shares(count, rows * top, most, lean, False)
    places = jnp.arange(count)

    def named(sizes, rotation):
        used = int((sizes > 0).sum())
        fixed = max(1, used // 4)
        shifted = fixed + (places - fixed + rotation * (used - fixed)) % max(1, count - fixed)
        return jnp.zeros((count,), jnp.int32).at[sequence[jnp.where(places < fixed, places, shifted)]].set(jnp.asarray(sizes, jnp.int32))

    sizes = jnp.where(number % 4 == 0, named(heavy_load, number // 4), named(common, number - number // 4 - 1))
    mixed = jax.random.permutation(jax.random.fold_in(own, 3), count)
    donor, taker = mixed[0:count // 2 * 2:2], mixed[1:count // 2 * 2:2]
    margin = jnp.minimum(sizes[donor] - 1, most - sizes[taker]) // 2
    margin = jnp.where((donor == sequence[0]) | (taker == sequence[0]) | (sizes[taker] == 0), 0, jnp.maximum(margin, 0))
    shifted = jax.random.randint(jax.random.fold_in(own, 4), (count // 2,), 0, 1 << 20) % (margin + 1)
    sizes = sizes.at[donor].add(-shifted).at[taker].add(shifted)
    labels = jnp.searchsorted(jnp.cumsum(sizes), jnp.arange(rows * top), side="right").astype(jnp.int32)
    table = labels.reshape(top, rows).T
    table = table[jax.random.permutation(jax.random.fold_in(own, 1), rows)]
    rotation = jax.random.randint(jax.random.fold_in(own, 2), (rows, 1), 0, top)
    return jnp.take_along_axis(table, (jnp.arange(top)[None, :] + rotation) % top, axis=1)


def load_shares(amount, total, most, lean, full):
    loads = [(1 << 20) // math.isqrt(grade ** lean) + 1 for grade in range(1, amount + 1)]
    largest = most if full else min(most, max(-(-total // amount), total * loads[0] // sum(loads)))
    least = 1 if total - largest >= amount - 1 else 0
    given, spare = [largest] + [least] * (amount - 1), total - largest - least * (amount - 1)
    while spare > 0:
        movable = [i for i in range(1, amount) if given[i] < largest] or [i for i in range(1, amount) if given[i] < most]
        pool, budget = sum([loads[i] for i in movable]), spare
        for i in movable:
            extra = min(most - given[i], max(1, budget * loads[i] // pool), spare)
            given[i] = given[i] + extra
            spare = spare - extra
    return np.array(given)


def normal_values(own_key, dims, deviation, reach, split=(), kind=jnp.bfloat16):
    loudness = level_of(own_key, dims, split, -0.22, 0.18) if split else 1.0
    entries = jax.random.normal(own_key, dims, jnp.float32) * deviation * loudness
    return jnp.minimum(jnp.maximum(entries, -reach), reach).astype(kind)


def setup_inputs(seed: int = 0) -> dict:
    arg_keys = jax.random.split(jax.random.key(seed), 19)
    tokens = normal_values(arg_keys[0], (SEQ, D), 1.0, 6.0, ((0, 8), (1, 16)))
    norm_gain = jnp.clip(1.0 + 0.1 * jax.random.normal(arg_keys[1], (D,), jnp.float32), 0.5, 1.5)
    in_x = normal_values(arg_keys[2], (D, INNER), D ** -0.5, 0.09375, ((0, 8), (1, 16)))
    in_z = normal_values(arg_keys[3], (D, INNER), D ** -0.5, 0.09375, ((0, 8), (1, 16)))
    conv_weight = normal_values(arg_keys[4], (CONV, INNER), CONV ** -0.5, 3.0, ((1, 16),), jnp.float32)
    conv_bias = jnp.clip(jax.random.uniform(arg_keys[5], (INNER,), jnp.float32, -0.5, 0.5) * level_of(arg_keys[5], (INNER,), ((0, 16),), -0.4, 0.0), -0.5, 0.5)
    xproj_weight = normal_values(arg_keys[6], (INNER, RANK + 2 * STATE), INNER ** -0.5, 0.046875, ((0, 16),))
    dt_weight = normal_values(arg_keys[7], (RANK, INNER), RANK ** -0.5, 0.25, ((1, 16),))
    dt_bias = jnp.clip(-6.0 + 4.0 * jax.random.uniform(arg_keys[8], (INNER,), jnp.float32) ** level_of(arg_keys[8], (INNER,), ((0, 16),), -0.2, 0.2), -6.0, -2.0)
    a_log = jnp.clip(-2.0 + 3.0 * jax.random.uniform(arg_keys[9], (INNER, STATE), jnp.float32) ** level_of(arg_keys[9], (INNER, STATE), ((0, 16),), -0.2, 0.2), -2.0, 1.0)
    skip_d = jnp.clip(0.5 + 1.0 * jax.random.uniform(arg_keys[10], (INNER,), jnp.float32) ** level_of(arg_keys[10], (INNER,), ((0, 16),), -0.2, 0.2), 0.5, 1.5)
    out_weight = normal_values(arg_keys[11], (INNER, D), INNER ** -0.5, 0.046875, ((0, 16), (1, 8)))
    moe_gain = jnp.clip(1.0 + 0.1 * jax.random.normal(arg_keys[12], (D,), jnp.float32), 0.5, 1.5)
    expert_ids_keys = jax.random.split(jax.random.fold_in(arg_keys[13], 1), SEQ // BLK)
    expert_ids_turns = jax.random.permutation(jax.random.fold_in(arg_keys[13], 3), SEQ // BLK)
    expert_ids = jax.vmap(lambda own, number: assign_block(jax.random.fold_in(arg_keys[13], 2), own, number, BLK, EXPERTS, TOPK, CAP, 2))(expert_ids_keys, expert_ids_turns).reshape((SEQ, TOPK))
    route_gates = jnp.clip(0.2 + 0.8 * jax.random.uniform(arg_keys[14], (SEQ, TOPK), jnp.float32) ** level_of(arg_keys[14], (SEQ, TOPK), ((0, 8),), -0.2, 0.2), 0.2, 1.0)
    w_gate = normal_values(arg_keys[15], (EXPERTS, D, FF), D ** -0.5, 0.09375, ((0, 8), (2, 16)))
    w_up = normal_values(arg_keys[16], (EXPERTS, D, FF), D ** -0.5, 0.09375, ((0, 8), (2, 16)))
    w_down = normal_values(arg_keys[17], (EXPERTS, FF, D), FF ** -0.5, 0.0546875, ((0, 8), (1, 16)))
    return {"tokens": tokens, "norm_gain": norm_gain, "in_x": in_x, "in_z": in_z, "conv_weight": conv_weight, "conv_bias": conv_bias, "xproj_weight": xproj_weight, "dt_weight": dt_weight, "dt_bias": dt_bias, "a_log": a_log, "skip_d": skip_d, "out_weight": out_weight, "moe_gain": moe_gain, "expert_ids": expert_ids, "route_gates": route_gates, "w_gate": w_gate, "w_up": w_up, "w_down": w_down}


EPS = 1e-05

def rms_scale(rows, gain):
    widened = rows.astype(jnp.float32)
    mean_sq = lax.optimization_barrier(jnp.mean(widened * widened, axis=-1, keepdims=True))
    return widened * lax.rsqrt(mean_sq + EPS) * gain

def link_pairs(earlier, later):
    return (earlier[0] * later[0], later[0] * earlier[1] + later[1])

def scan_block(step_block, input_block, rate_block, input_map, output_map):
    decays = jnp.exp(step_block[:, :, None] * rate_block[None, :, :])
    drive_term = (step_block * input_block)[:, :, None] * input_map[:, None, :]
    states = lax.associative_scan(link_pairs, (decays, drive_term), axis=0)[1]
    return jnp.einsum('tcn,tn->tc', states, output_map)

def expert_rows(rows, gate_w, up_w, down_w):
    gate_part = jnp.dot(rows, gate_w, preferred_element_type=jnp.float32)
    up_part = jnp.dot(rows, up_w, preferred_element_type=jnp.float32)
    active = (jax.nn.silu(gate_part) * up_part).astype(jnp.bfloat16)
    group = FF // N_TP
    total = jnp.zeros((rows.shape[0], D), jnp.float32)
    for index in range(N_TP):
        part = jnp.dot(active[:, index * group:(index + 1) * group], down_w[index * group:(index + 1) * group], preferred_element_type=jnp.float32)
        total = total + part.astype(jnp.bfloat16).astype(jnp.float32)
    return total

def reference(tokens, norm_gain, in_x, in_z, conv_weight, conv_bias, xproj_weight, dt_weight, dt_bias, a_log, skip_d, out_weight, moe_gain, expert_ids, route_gates, w_gate, w_up, w_down):
    normed = rms_scale(tokens, norm_gain).astype(jnp.bfloat16)
    inner_u = jnp.dot(normed, in_x, preferred_element_type=jnp.float32)
    inner_z = jnp.dot(normed, in_z, preferred_element_type=jnp.float32)
    extended = jnp.concatenate([jnp.zeros((CONV - 1, INNER), jnp.float32), inner_u], axis=0)
    conv_sum = conv_bias + jnp.zeros((SEQ, INNER), jnp.float32)
    for offset in range(CONV):
        conv_sum = conv_sum + conv_weight[offset] * extended[offset:offset + SEQ]
    mixed_in = jax.nn.silu(conv_sum)
    projected = jnp.dot(mixed_in.astype(jnp.bfloat16), xproj_weight, preferred_element_type=jnp.float32)
    dt_low = projected[:, :RANK].astype(jnp.bfloat16)
    input_map = projected[:, RANK:RANK + STATE]
    output_map = projected[:, RANK + STATE:]
    step_size = jax.nn.softplus(jnp.dot(dt_low, dt_weight, preferred_element_type=jnp.float32) + dt_bias)
    decay_rate = -jnp.exp(a_log)
    group = INNER // N_TP
    steps_grouped = step_size.reshape(SEQ, N_TP, group).transpose(1, 0, 2)
    inputs_grouped = mixed_in.reshape(SEQ, N_TP, group).transpose(1, 0, 2)
    rates_grouped = decay_rate.reshape(N_TP, group, STATE)

    def one_group(packed):
        return scan_block(packed[0], packed[1], packed[2], input_map, output_map)
    scanned = lax.map(one_group, (steps_grouped, inputs_grouped, rates_grouped))
    scan_out = scanned.transpose(1, 0, 2).reshape(SEQ, INNER) + skip_d * mixed_in
    gated_rows = (scan_out * jax.nn.silu(inner_z)).astype(jnp.bfloat16)
    mixer_out = jnp.dot(gated_rows, out_weight, preferred_element_type=jnp.float32)
    resid = (tokens.astype(jnp.float32) + mixer_out).astype(jnp.bfloat16)
    normed_moe = rms_scale(resid, moe_gain).astype(jnp.bfloat16)
    routes = expert_ids.reshape(N_SECTION, BLK * TOPK)
    expert_range = jnp.arange(EXPERTS, dtype=jnp.int32)
    one_hot = (routes[:, :, None] == expert_range[None, None, :]).astype(jnp.int32)
    earlier_count = (jnp.cumsum(one_hot, axis=1) - one_hot).astype(jnp.int32)
    slot_index = lax.optimization_barrier(jnp.sum(earlier_count * one_hot, axis=2)).astype(jnp.int32)
    section_index = jnp.arange(N_SECTION, dtype=jnp.int32)[:, None]
    table_row = (routes * (N_SECTION * CAP) + section_index * CAP + slot_index).reshape(-1).astype(jnp.int32)
    token_index = (section_index * BLK + jnp.arange(BLK * TOPK, dtype=jnp.int32)[None, :] // TOPK).reshape(-1).astype(jnp.int32)
    table_size = EXPERTS * N_SECTION * CAP
    row_token = jnp.zeros((table_size,), jnp.int32).at[table_row].set(token_index)
    row_filled = jnp.zeros((table_size,), jnp.int32).at[table_row].set(jnp.ones_like(token_index))
    gathered = jnp.where(row_filled[:, None] > 0, normed_moe[row_token], jnp.zeros((), jnp.bfloat16))
    gathered = gathered.reshape(EXPERTS, N_SECTION * CAP, D)

    def one_expert(packed):
        return expert_rows(packed[0], packed[1], packed[2], packed[3])
    outputs = lax.map(one_expert, (gathered, w_gate, w_up, w_down))
    picked = outputs.reshape(table_size, D)[table_row].reshape(SEQ, TOPK, D)
    moe_sum = lax.optimization_barrier(jnp.sum(picked * route_gates[:, :, None], axis=1))
    return (resid.astype(jnp.float32) + moe_sum).astype(jnp.bfloat16)
```

```python
import jax
import jax.numpy as jnp
from jax import lax
from jax.experimental import pallas as pl
from jax.experimental.pallas import tpu as pltpu
from jax.sharding import Mesh, PartitionSpec as P

EPS = 1e-05
BF = jnp.bfloat16
F32 = jnp.float32
LOG2E = 1.4426950408889634
HALO = 8


def shift(v, axis, d):
    n = lax.axis_size(axis)
    return lax.ppermute(v, axis, [(i, (i + d) % n) for i in range(n)])


def gather_rel(v, axis):
    return [v] + [shift(v, axis, d) for d in range(1, lax.axis_size(axis))]


def pick(stacked, index):
    return lax.dynamic_index_in_dim(stacked, index, 0, keepdims=False)


def total(terms):
    out = terms[0].astype(F32)
    for term in terms[1:]:
        out = out + term.astype(F32)
    return out


def swap_xz(v):
    return lax.ppermute(v, ("x", "z"), [(4 * i + j, 4 * j + i) for i in range(4) for j in range(4)])


def softplus(v):
    return jnp.maximum(v, 0.0) + jnp.log1p(jnp.exp(-jnp.abs(v)))


def silu(v):
    return v / (1.0 + jnp.exp(-v))


def state_kernel(maps_ref, step_ref, drive_ref, rate_ref, out_ref):
    steps, states = step_ref.shape[0], rate_ref.shape[0]
    rates = [rate_ref[n] for n in range(states)]

    def body(t, carry):
        h, acc = carry
        st, du = step_ref[t], drive_ref[t]
        h = tuple(
            h[n] * jnp.exp2(st * rates[n]) + du * maps_ref[t * 2 * states + n] for n in range(states)
        )
        return h, acc + st

    zero = jnp.zeros(step_ref.shape[1:], F32)
    h, acc = lax.fori_loop(0, steps, body, ((zero,) * states, zero), unroll=2)
    for n in range(states):
        out_ref[n] = h[n].astype(BF)
    high = acc.astype(BF)
    out_ref[states] = high
    out_ref[states + 1] = (acc - high.astype(F32)).astype(BF)


def scan_kernel(place_ref, maps_ref, step_ref, drive_ref, rate_ref, same_ref, other_ref, out_ref):
    steps, states = step_ref.shape[0], rate_ref.shape[0]
    rates = [rate_ref[n] for n in range(states)]
    x, core = place_ref[0], place_ref[1]
    section = 2 * x + core
    zero = jnp.zeros(step_ref.shape[1:], F32)

    def join(earlier, h):
        slot = lax.rem(x - earlier // 2 + 4, 4)
        mine = lax.rem(earlier, 2) == core

        def entry(n):
            return jnp.where(mine, same_ref[slot, n].astype(F32), other_ref[slot, n].astype(F32))

        acc = entry(states) + entry(states + 1)
        return tuple(h[n] * jnp.exp2(acc * rates[n]) + entry(n) for n in range(states))

    h = lax.fori_loop(0, section, join, (zero,) * states)

    def body(t, h):
        st, du = step_ref[t], drive_ref[t]
        base = t * 2 * states
        h = tuple(h[n] * jnp.exp2(st * rates[n]) + du * maps_ref[base + n] for n in range(states))
        terms = [h[n] * maps_ref[base + states + n] for n in range(states)]
        while len(terms) > 1:
            terms = [a + b for a, b in zip(terms[::2], terms[1::2])]
        out_ref[t] = terms[0]
        return h

    lax.fori_loop(0, steps, body, h, unroll=2)


def local_state(maps, step, drive, rate):
    states = rate.shape[0]
    return pl.pallas_call(
        state_kernel,
        out_shape=jax.ShapeDtypeStruct((states + 2,) + step.shape[1:], BF),
        in_specs=[pl.BlockSpec(memory_space=pltpu.SMEM)] + [pl.BlockSpec(memory_space=pltpu.VMEM)] * 3,
        out_specs=pl.BlockSpec(memory_space=pltpu.VMEM),
        name="local_state",
    )(maps, step, drive, rate)


def full_scan(place, maps, step, drive, rate, same, other):
    return pl.pallas_call(
        scan_kernel,
        out_shape=jax.ShapeDtypeStruct(step.shape, F32),
        in_specs=[pl.BlockSpec(memory_space=pltpu.SMEM)] * 2 + [pl.BlockSpec(memory_space=pltpu.VMEM)] * 5,
        out_specs=pl.BlockSpec(memory_space=pltpu.VMEM),
        name="full_scan",
    )(place, maps, step, drive, rate, same, other)


def shards(
    tokens,
    norm_gain,
    in_x,
    in_z,
    conv_weight,
    conv_bias,
    xproj_weight,
    dt_weight,
    dt_bias,
    a_log,
    skip_d,
    out_weight,
    moe_gain,
    expert_ids,
    route_gates,
    w_gate,
    w_up,
    w_down,
):
    x, core, z, y = (lax.axis_index(a) for a in ("x", "core", "z", "y"))
    block_rows, col_share = tokens.shape
    width = norm_gain.shape[0]
    channels = in_x.shape[1]
    lanes = channels // 8
    rank = dt_weight.shape[0]
    states = a_log.shape[1]
    swap_cores = [(0, 1), (1, 0)]

    own = swap_xz(tokens)
    behind = []
    for xd in range(4):
        for cd in range(2):
            for zd in range(4):
                for yd in range(4):
                    before = 2 * zd + cd - 1
                    if before >= 0:
                        src = ((before // 2 * 2 + before % 2) * 4 + xd) * 4 + yd
                        behind.append((src, ((xd * 2 + cd) * 4 + zd) * 4 + yd))
    tail = lax.ppermute(tokens[block_rows - HALO :], ("x", "core", "z", "y"), behind)
    ext = jnp.concatenate([tail, own], axis=0)
    ext_rows = ext.shape[0]

    def feature_rows(w):
        far = lax.ppermute(w, "core", swap_cores)
        both = jnp.where(core == 0, jnp.stack([w, far]), jnp.stack([far, w]))
        both = both.reshape(4, col_share, w.shape[1])
        gains = lax.dynamic_slice_in_dim(norm_gain, x * 4 * col_share, 4 * col_share).reshape(4, col_share, 1)
        scaled = (both.astype(F32) * gains).astype(BF)
        return jnp.concatenate([pick(scaled, (y - j + 4) % 4) for j in range(4)], axis=0)

    weight_x = feature_rows(in_x)
    weight_z = feature_rows(in_z)

    wide = jnp.concatenate(gather_rel(ext, "y"), axis=1)
    rows = jnp.concatenate(gather_rel(wide, "z"), axis=0)
    raw = rows.astype(F32)
    square_sum = jnp.sum(raw * raw, axis=1).reshape(4, 1, ext_rows)
    square_high = square_sum.astype(BF)
    square_low = (square_sum - square_high.astype(F32)).astype(BF)
    part_u = jnp.dot(rows, weight_x, preferred_element_type=F32).astype(BF).reshape(4, ext_rows, channels)
    pad = ((0, 0), (0, 0), (0, channels - ext_rows))
    part_u = jnp.concatenate(
        [jnp.pad(square_high, pad), jnp.pad(square_low, pad), part_u[:, 2:]], axis=1
    )
    rows_z = rows.reshape(4, ext_rows, -1)[:, HALO:].reshape(4 * block_rows, -1)
    part_z = jnp.dot(rows_z, weight_z, preferred_element_type=F32).astype(BF).reshape(4, block_rows, channels)

    def over_x(part):
        return total([pick(part, (z - x + 4) % 4)] + [shift(pick(part, (z - x - d + 8) % 4), "x", d) for d in range(1, 4)])

    sum_u = over_x(part_u)
    sum_z = over_x(part_z)
    mean_sq = (sum_u[0, :ext_rows] + sum_u[1, :ext_rows]) / width
    scale = lax.rsqrt(mean_sq + EPS)[:, None]
    inner_u = sum_u * scale
    inner_z = sum_z * scale[HALO:]

    taps = conv_weight.shape[0]
    conv_sum = conv_bias + jnp.zeros((block_rows, channels), F32)
    for offset in range(taps):
        start = HALO - (taps - 1) + offset
        conv_sum = conv_sum + conv_weight[offset] * inner_u[start : start + block_rows]
    mixed_in = silu(conv_sum)

    part_p = jnp.dot(mixed_in.astype(BF), xproj_weight, preferred_element_type=F32).astype(BF)
    part_p = part_p.reshape(4, block_rows // 4, -1)
    some = total([pick(part_p, y)] + [shift(pick(part_p, (y + d) % 4), "y", d) for d in range(1, 4)]).astype(BF)
    some = total(gather_rel(some, "z")).astype(BF)
    some = jnp.stack(gather_rel(some, "y"))
    projected = jnp.concatenate([pick(some, (y - j + 4) % 4) for j in range(4)], axis=0)

    dt_low = projected[:, :rank]
    maps = projected[:, rank:].astype(F32).reshape(-1)
    step = softplus(jnp.dot(dt_low, dt_weight, preferred_element_type=F32) + dt_bias)
    drive = step * mixed_in
    rate = (-jnp.exp(a_log) * LOG2E).T.reshape(states, 8, lanes)
    step3 = step.reshape(block_rows, 8, lanes)
    drive3 = drive.reshape(block_rows, 8, lanes)
    ends = local_state(maps, step3, drive3, rate)
    same = jnp.stack(gather_rel(ends, "x"))
    other = lax.ppermute(same, "core", swap_cores)
    place = jnp.stack([x, core]).astype(jnp.int32)
    scanned = full_scan(place, maps, step3, drive3, rate, same, other).reshape(block_rows, channels)
    gated = ((scanned + skip_d * mixed_in) * silu(inner_z)).astype(BF)

    far_out = lax.ppermute(out_weight, "core", swap_cores)
    out_both = jnp.where(
        core == 0,
        jnp.concatenate([out_weight, far_out], axis=1),
        jnp.concatenate([far_out, out_weight], axis=1),
    )
    gated_rows = jnp.concatenate(gather_rel(gated, "x"), axis=0)
    part_o = jnp.dot(gated_rows, out_both, preferred_element_type=F32).astype(BF).reshape(4, block_rows, -1)
    sum_o = total(
        [pick(part_o, (x - z + 4) % 4)] + [shift(pick(part_o, (x - z - d + 8) % 4), "z", d) for d in range(1, 4)]
    ).astype(BF)
    sum_o = sum_o.reshape(block_rows, 4, col_share).transpose(1, 0, 2)
    mixer = total([pick(sum_o, y)] + [shift(pick(sum_o, (y + d) % 4), "y", d) for d in range(1, 4)])
    resid = (own.astype(F32) + mixer).astype(BF)

    routing = swap_xz(jnp.concatenate([expert_ids.astype(F32).T, route_gates.T], axis=0))
    top = expert_ids.shape[1]
    experts = lax.axis_size("x") * lax.axis_size("core")
    capacity = block_rows * top * 3 // (2 * experts)
    flat_ids = routing[:top].reshape(-1).astype(jnp.int32)
    gates = routing[top:]
    one_hot = flat_ids[:, None] == jnp.arange(experts, dtype=jnp.int32)[None, :]
    flat = jnp.arange(block_rows * top, dtype=jnp.int32)
    before = (flat[:, None] > flat[None, :]).astype(BF)
    earlier = jnp.dot(before, one_hot.astype(BF), preferred_element_type=F32)
    slot = jnp.sum(jnp.where(one_hot, earlier, 0.0), axis=1).astype(jnp.int32)
    dest = flat_ids * capacity + slot
    cells = jnp.arange(experts * capacity, dtype=jnp.int32)
    place_of = dest[:, None] == cells[None, :]
    send = (place_of[:block_rows] | place_of[block_rows:]).astype(BF)
    outgoing = lax.dot_general(send, resid, (((0,), (0,)), ((), ())), preferred_element_type=F32).astype(BF)
    received = lax.all_to_all(
        outgoing.reshape(experts, capacity, col_share), ("x", "core"), 0, 0, tiled=True
    )
    block = received.reshape(4, 2, capacity, col_share).transpose(1, 2, 0, 3)
    block = jnp.stack(gather_rel(block, "y"))
    block = jnp.stack([pick(block, (y - j + 4) % 4) for j in range(4)], axis=3)
    block = block.reshape(2 * capacity, width).astype(F32)
    mean_sq = jnp.mean(block * block, axis=-1, keepdims=True)
    block = (block * lax.rsqrt(mean_sq + EPS) * moe_gain).astype(BF)
    batch = jnp.concatenate(gather_rel(block, "z"), axis=0)
    gate_part = jnp.dot(batch, w_gate[0], preferred_element_type=F32)
    up_part = jnp.dot(batch, w_up[0], preferred_element_type=F32)
    active = (silu(gate_part) * up_part).astype(BF)
    result = jnp.dot(active, w_down[0], preferred_element_type=F32).astype(BF)
    result = result.reshape(4, 2 * capacity, width)
    back = total([result[0]] + [shift(result[k], "z", 4 - k) for k in range(1, 4)]).astype(BF)
    back = back.reshape(2, capacity, 4, 4, col_share).transpose(3, 2, 0, 1, 4)
    back = total([pick(back, y)] + [shift(pick(back, (y + d) % 4), "y", d) for d in range(1, 4)]).astype(BF)
    returned = lax.all_to_all(
        back.reshape(experts, capacity, col_share), ("x", "core"), 0, 0, tiled=True
    ).reshape(experts * capacity, col_share)
    picked = jnp.dot(place_of.astype(BF), returned, preferred_element_type=F32)
    moe = picked[:block_rows] * gates[0][:, None] + picked[block_rows:] * gates[1][:, None]
    return swap_xz((resid.astype(F32) + moe).astype(BF))


def solution(mesh):
    fine = Mesh(mesh.devices.reshape(4, 2, 4, 4), ("x", "core", "z", "y"))
    section, tp = ("x", "core"), ("z", "y")
    placed = (
        P(section, tp),
        P(),
        P(section, tp),
        P(section, tp),
        P(None, tp),
        P(tp),
        P(tp, None),
        P(None, tp),
        P(tp),
        P(tp, None),
        P(tp),
        P(tp, section),
        P(),
        P(section, None),
        P(section, None),
        P(section, None, tp),
        P(section, None, tp),
        P(section, tp, None),
    )
    return jax.shard_map(
        shards, mesh=fine, in_specs=placed, out_specs=P(section, tp), check_vma=False
    )
```

```python
import jax
import jax.numpy as jnp
from jax import lax
from jax.experimental import pallas as pl
from jax.experimental.pallas import tpu as pltpu
from jax.sharding import Mesh, PartitionSpec as P

EPS = 1e-05
BF = jnp.bfloat16
F32 = jnp.float32
LOG2E = 1.4426950408889634
HALO = 8


def shift(v, axis, d):
    n = lax.axis_size(axis)
    return lax.ppermute(v, axis, [(i, (i + d) % n) for i in range(n)])


def gather_rel(v, axis):
    return [v] + [shift(v, axis, d) for d in range(1, lax.axis_size(axis))]


def pick(stacked, index):
    return lax.dynamic_index_in_dim(stacked, index, 0, keepdims=False)


def total(terms):
    out = terms[0].astype(F32)
    for term in terms[1:]:
        out = out + term.astype(F32)
    return out


def swap_xz(v):
    return lax.ppermute(v, ("x", "z"), [(4 * i + j, 4 * j + i) for i in range(4) for j in range(4)])


def softplus(v):
    return jnp.maximum(v, 0.0) + jnp.log1p(jnp.exp(-jnp.abs(v)))


def silu(v):
    return v / (1.0 + jnp.exp(-v))


def state_kernel(maps_ref, step_ref, drive_ref, rate_ref, out_ref):
    steps, states = step_ref.shape[0], rate_ref.shape[0]
    rates = [rate_ref[n] for n in range(states)]

    def body(t, carry):
        h, acc = carry
        st, du = step_ref[t], drive_ref[t]
        h = tuple(
            h[n] * jnp.exp2(st * rates[n]) + du * maps_ref[t * 2 * states + n] for n in range(states)
        )
        return h, acc + st

    zero = jnp.zeros(step_ref.shape[1:], F32)
    h, acc = lax.fori_loop(0, steps, body, ((zero,) * states, zero), unroll=2)
    for n in range(states):
        out_ref[n] = h[n].astype(BF)
    high = acc.astype(BF)
    out_ref[states] = high
    out_ref[states + 1] = (acc - high.astype(F32)).astype(BF)


def scan_kernel(place_ref, maps_ref, step_ref, drive_ref, rate_ref, same_ref, other_ref, out_ref):
    steps, states = step_ref.shape[0], rate_ref.shape[0]
    rates = [rate_ref[n] for n in range(states)]
    x, core = place_ref[0], place_ref[1]
    section = 2 * x + core
    zero = jnp.zeros(step_ref.shape[1:], F32)

    def join(earlier, h):
        slot = lax.rem(x - earlier // 2 + 4, 4)
        mine = lax.rem(earlier, 2) == core

        def entry(n):
            return jnp.where(mine, same_ref[slot, n].astype(F32), other_ref[slot, n].astype(F32))

        acc = entry(states) + entry(states + 1)
        return tuple(h[n] * jnp.exp2(acc * rates[n]) + entry(n) for n in range(states))

    h = lax.fori_loop(0, section, join, (zero,) * states)

    def body(t, h):
        st, du = step_ref[t], drive_ref[t]
        base = t * 2 * states
        h = tuple(h[n] * jnp.exp2(st * rates[n]) + du * maps_ref[base + n] for n in range(states))
        terms = [h[n] * maps_ref[base + states + n] for n in range(states)]
        while len(terms) > 1:
            terms = [a + b for a, b in zip(terms[::2], terms[1::2])]
        out_ref[t] = terms[0]
        return h

    lax.fori_loop(0, steps, body, h, unroll=2)


def local_state(maps, step, drive, rate):
    states = rate.shape[0]
    return pl.pallas_call(
        state_kernel,
        out_shape=jax.ShapeDtypeStruct((states + 2,) + step.shape[1:], BF),
        in_specs=[pl.BlockSpec(memory_space=pltpu.SMEM)] + [pl.BlockSpec(memory_space=pltpu.VMEM)] * 3,
        out_specs=pl.BlockSpec(memory_space=pltpu.VMEM),
        name="local_state",
    )(maps, step, drive, rate)


def full_scan(place, maps, step, drive, rate, same, other):
    return pl.pallas_call(
        scan_kernel,
        out_shape=jax.ShapeDtypeStruct(step.shape, F32),
        in_specs=[pl.BlockSpec(memory_space=pltpu.SMEM)] * 2 + [pl.BlockSpec(memory_space=pltpu.VMEM)] * 5,
        out_specs=pl.BlockSpec(memory_space=pltpu.VMEM),
        name="full_scan",
    )(place, maps, step, drive, rate, same, other)


def expert_kernel(place_ref, gain_ref, *refs):
    first, second, (gate_ref, up_ref, down_ref) = refs[:4], refs[4:8], refs[8:11]
    first_out, second_out, (batch, active) = refs[11:15], refs[15:19], refs[19:]
    step = pl.program_id(0)
    hidden = gate_ref.shape[1]
    gate_steps = active.shape[1] // hidden
    _, count, wide = first[0].shape
    share = wide // 4
    width = batch.shape[1]
    y = place_ref[0]
    pieces = [(k, j) for k in range(4) for j in range(4)]

    def column(j):
        return lax.rem(y - j + 4, 4)

    @pl.when(step == 0)
    def _():
        for half, source in enumerate((first, second)):
            for k in range(4):
                blocks = [(source[k][j] if half == 0 else source[j][k]).astype(F32) for j in range(4)]
                square = sum(jnp.sum(b * b, axis=1, keepdims=True) for b in blocks)
                scale = lax.rsqrt(square / width + EPS)
                top = (half * 4 + k) * count
                for j in range(4):
                    for i in range(4):
                        at = pl.multiple_of(i * wide + column(j) * share, share)
                        piece = blocks[j][:, i * share : (i + 1) * share] * scale * gain_ref[:, pl.ds(at, share)]
                        batch[pl.ds(top, count), pl.ds(at, share)] = piece.astype(BF)

    for number in range(gate_steps):

        @pl.when(step == number)
        def _():
            rows = batch[...]
            gate = jnp.dot(rows, gate_ref[...], preferred_element_type=F32)
            up = jnp.dot(rows, up_ref[...], preferred_element_type=F32)
            active[:, number * hidden : (number + 1) * hidden] = (silu(gate) * up).astype(BF)

    for number in range(4):

        @pl.when(step == gate_steps + number)
        def _():
            out = jnp.dot(active[...], down_ref[...], preferred_element_type=F32).astype(BF)
            for i in range(4):
                columns = out[:, i * share : (i + 1) * share]
                to = lax.rem(y - i + 4, 4)
                for k in range(4):
                    rows = slice(k * count, (k + 1) * count)
                    first_out[k][to, :, number * share : (number + 1) * share] = columns[rows]
                rows = slice(4 * count, 8 * count)
                for j in range(4):

                    @pl.when(to == j)
                    def _():
                        second_out[j][:, :, number * share : (number + 1) * share] = columns[rows].reshape(
                            4, count, share
                        )


def expert_block(place, gain, first, second, w_gate, w_up, w_down):
    width, hidden = w_gate.shape
    tile = 256
    gate_steps = hidden // tile
    _, count, wide = first[0].shape
    block = pl.BlockSpec((4, count, wide), lambda i: (0, 0, 0))
    into = pl.BlockSpec((width, tile), lambda i: (0, jnp.minimum(i, gate_steps - 1)))
    return pl.pallas_call(
        expert_kernel,
        grid=(gate_steps + 4,),
        out_shape=[jax.ShapeDtypeStruct((4, count, wide), BF)] * 8,
        in_specs=[pl.BlockSpec(memory_space=pltpu.SMEM), pl.BlockSpec((1, width), lambda i: (0, 0))]
        + [block] * 8
        + [into, into, pl.BlockSpec((hidden, wide), lambda i: (0, jnp.maximum(i - gate_steps, 0)))],
        out_specs=[block] * 8,
        scratch_shapes=[pltpu.VMEM((8 * count, width), BF), pltpu.VMEM((8 * count, hidden), BF)],
        compiler_params=pltpu.CompilerParams(vmem_limit_bytes=48 * 1024 * 1024),
        cost_estimate=pl.CostEstimate(
            flops=48 * count * width * hidden, bytes_accessed=6 * width * hidden, transcendentals=8 * count * hidden
        ),
        name="expert_block",
    )(place, gain.reshape(1, -1), *first, *second, w_gate, w_up, w_down)


def shards(
    tokens,
    norm_gain,
    in_x,
    in_z,
    conv_weight,
    conv_bias,
    xproj_weight,
    dt_weight,
    dt_bias,
    a_log,
    skip_d,
    out_weight,
    moe_gain,
    expert_ids,
    route_gates,
    w_gate,
    w_up,
    w_down,
):
    x, core, z, y = (lax.axis_index(a) for a in ("x", "core", "z", "y"))
    block_rows, col_share = tokens.shape
    width = norm_gain.shape[0]
    channels = in_x.shape[1]
    lanes = channels // 8
    rank = dt_weight.shape[0]
    states = a_log.shape[1]
    swap_cores = [(0, 1), (1, 0)]

    own = swap_xz(tokens)
    gains = lax.dynamic_slice_in_dim(norm_gain, x * 4 * col_share, 4 * col_share).reshape(4, col_share)
    gained = (own.astype(F32) * pick(gains, y)).astype(BF)

    order = [(2 * core + i) % 4 for i in range(4)]
    parts = jnp.stack(gather_rel(gained, "y"))
    wide = jnp.concatenate([pick(parts, (y - o + 4) % 4) for o in order], axis=1)
    rows = jnp.concatenate(gather_rel(wide, "z"), axis=0)
    ends_far = lax.ppermute(
        jnp.concatenate([rows[(k + 1) * block_rows - HALO : (k + 1) * block_rows] for k in range(4)], axis=0),
        "core",
        swap_cores,
    ).reshape(4, HALO, -1)
    far_x = lax.ppermute(in_x, "core", swap_cores)
    far_z = lax.ppermute(in_z, "core", swap_cores)
    half = in_x.shape[0]

    def project(v, near, far, swapped=False):
        first, second = v[:, :half], v[:, half:]
        if swapped:
            first, second = second, first
        return jnp.dot(first, near, preferred_element_type=F32) + jnp.dot(second, far, preferred_element_type=F32)

    later = jnp.where(
        (jnp.arange(4) == z)[:, None, None], jnp.zeros((), BF), jnp.roll(ends_far, -1, axis=0)
    )
    tail = jnp.where(core == 0, later, ends_far).reshape(4 * HALO, -1)
    inverse = 1.0 / jnp.concatenate([pick(gains, o) for o in order])

    def squares(v, inv):
        raw = v.astype(F32) * inv
        return jnp.sum(raw * raw, axis=1)

    square_sum = jnp.concatenate(
        [
            squares(tail, jnp.roll(inverse, half)).reshape(4, 1, HALO),
            squares(rows, inverse).reshape(4, 1, block_rows),
        ],
        axis=2,
    )
    ext_rows = HALO + block_rows
    square_high = square_sum.astype(BF)
    square_low = (square_sum - square_high.astype(F32)).astype(BF)
    part_tail = project(tail, in_x, far_x, True).astype(BF).reshape(4, HALO, channels)
    part_u = project(rows, in_x, far_x).astype(BF).reshape(4, block_rows, channels)
    pad = ((0, 0), (0, 0), (0, channels - ext_rows))
    part_u = jnp.concatenate(
        [jnp.pad(square_high, pad), jnp.pad(square_low, pad), part_tail[:, 2:], part_u], axis=1
    )
    part_z = project(rows, in_z, far_z).astype(BF).reshape(4, block_rows, channels)

    def over_x(part):
        return total([pick(part, (z - x + 4) % 4)] + [shift(pick(part, (z - x - d + 8) % 4), "x", d) for d in range(1, 4)])

    sum_u = over_x(part_u)
    sum_z = over_x(part_z)
    mean_sq = (sum_u[0, :ext_rows] + sum_u[1, :ext_rows]) / width
    scale = lax.rsqrt(mean_sq + EPS)[:, None]
    inner_u = sum_u * scale
    inner_z = sum_z * scale[HALO:]

    taps = conv_weight.shape[0]
    conv_sum = conv_bias + jnp.zeros((block_rows, channels), F32)
    for offset in range(taps):
        start = HALO - (taps - 1) + offset
        conv_sum = conv_sum + conv_weight[offset] * inner_u[start : start + block_rows]
    mixed_in = silu(conv_sum)

    part_p = jnp.dot(mixed_in.astype(BF), xproj_weight, preferred_element_type=F32).astype(BF)
    projected = total(gather_rel(part_p, "y")).astype(BF)
    projected = total(gather_rel(projected, "z")).astype(BF)

    dt_low = projected[:, :rank]
    maps = projected[:, rank:].astype(F32).reshape(-1)
    step = softplus(jnp.dot(dt_low, dt_weight, preferred_element_type=F32) + dt_bias)
    drive = step * mixed_in
    rate = (-jnp.exp(a_log) * LOG2E).T.reshape(states, 8, lanes)
    step3 = step.reshape(block_rows, 8, lanes)
    drive3 = drive.reshape(block_rows, 8, lanes)
    ends = local_state(maps, step3, drive3, rate)
    same = jnp.stack(gather_rel(ends, "x"))
    other = lax.ppermute(same, "core", swap_cores)
    place = jnp.stack([x, core]).astype(jnp.int32)
    scanned = full_scan(place, maps, step3, drive3, rate, same, other).reshape(block_rows, channels)
    gated = ((scanned + skip_d * mixed_in) * silu(inner_z)).astype(BF)

    far_out = lax.ppermute(out_weight, "core", swap_cores)
    out_both = jnp.where(
        core == 0,
        jnp.concatenate([out_weight, far_out], axis=1),
        jnp.concatenate([far_out, out_weight], axis=1),
    )
    gated_rows = jnp.concatenate(gather_rel(gated, "x"), axis=0)
    part_o = jnp.dot(gated_rows, out_both, preferred_element_type=F32).astype(BF).reshape(4, block_rows, -1)
    sum_o = total(
        [pick(part_o, (x - z + 4) % 4)] + [shift(pick(part_o, (x - z - d + 8) % 4), "z", d) for d in range(1, 4)]
    ).astype(BF)
    sum_o = sum_o.reshape(block_rows, 4, col_share).transpose(1, 0, 2)
    mixer = total([pick(sum_o, y)] + [shift(pick(sum_o, (y + d) % 4), "y", d) for d in range(1, 4)])
    resid = (own.astype(F32) + mixer).astype(BF)

    routing = swap_xz(jnp.concatenate([expert_ids.astype(F32).T, route_gates.T], axis=0))
    top = expert_ids.shape[1]
    experts = lax.axis_size("x") * lax.axis_size("core")
    capacity = block_rows * top * 3 // (2 * experts)
    flat_ids = routing[:top].reshape(-1).astype(jnp.int32)
    gates = routing[top:]
    one_hot = flat_ids[:, None] == jnp.arange(experts, dtype=jnp.int32)[None, :]
    flat = jnp.arange(block_rows * top, dtype=jnp.int32)
    before = (flat[:, None] > flat[None, :]).astype(BF)
    earlier = jnp.dot(before, one_hot.astype(BF), preferred_element_type=F32)
    slot = jnp.sum(jnp.where(one_hot, earlier, 0.0), axis=1).astype(jnp.int32)
    dest = flat_ids * capacity + slot
    cells = jnp.arange(experts * capacity, dtype=jnp.int32)
    place_of = dest[:, None] == cells[None, :]
    send = (place_of[:block_rows] | place_of[block_rows:]).astype(BF)
    outgoing = lax.dot_general(send, resid, (((0,), (0,)), ((), ())), preferred_element_type=F32).astype(BF)
    received = lax.all_to_all(
        outgoing.reshape(experts, capacity, col_share), ("x", "core"), 0, 0, tiled=True
    )
    halves = received.reshape(4, 2, capacity, col_share).transpose(1, 2, 0, 3).reshape(2, capacity, -1)
    first = gather_rel(jnp.stack(gather_rel(halves[0], "y")), "z")
    second = gather_rel(jnp.stack(gather_rel(halves[1], "z")), "y")
    sums = expert_block(y.astype(jnp.int32).reshape(1), moe_gain, first, second, w_gate[0], w_up[0], w_down[0])

    def home(blocks, early, late):
        some = total([blocks[0]] + [shift(blocks[k], early, 4 - k) for k in range(1, 4)]).astype(BF)
        return total([some[0]] + [shift(some[k], late, 4 - k) for k in range(1, 4)]).astype(BF)

    back = jnp.stack([home(sums[:4], "z", "y"), home(sums[4:], "y", "z")])
    back = back.reshape(2, capacity, 4, col_share).transpose(2, 0, 1, 3)
    returned = lax.all_to_all(
        back.reshape(experts, capacity, col_share), ("x", "core"), 0, 0, tiled=True
    ).reshape(experts * capacity, col_share)
    picked = jnp.dot(place_of.astype(BF), returned, preferred_element_type=F32)
    moe = picked[:block_rows] * gates[0][:, None] + picked[block_rows:] * gates[1][:, None]
    return swap_xz((resid.astype(F32) + moe).astype(BF))


def solution(mesh):
    fine = Mesh(mesh.devices.reshape(4, 2, 4, 4), ("x", "core", "z", "y"))
    section, tp = ("x", "core"), ("z", "y")
    placed = (
        P(section, tp),
        P(),
        P(section, tp),
        P(section, tp),
        P(None, tp),
        P(tp),
        P(tp, None),
        P(None, tp),
        P(tp),
        P(tp, None),
        P(tp),
        P(tp, section),
        P(),
        P(section, None),
        P(section, None),
        P(section, None, tp),
        P(section, None, tp),
        P(section, tp, None),
    )
    return jax.shard_map(
        shards, mesh=fine, in_specs=placed, out_specs=P(section, tp), check_vma=False
    )
```

```python
import jax
import jax.numpy as jnp
from jax import lax
from jax.experimental import pallas as pl
from jax.experimental.pallas import tpu as pltpu
from jax.sharding import Mesh, PartitionSpec as P

EPS = 1e-05
BF = jnp.bfloat16
F32 = jnp.float32
LOG2E = 1.4426950408889634
HALO = 16


def shift(v, axis, d):
    n = lax.axis_size(axis)
    return lax.ppermute(v, axis, [(i, (i + d) % n) for i in range(n)])


def gather_rel(v, axis):
    return [v] + [shift(v, axis, d) for d in range(1, lax.axis_size(axis))]


def pick(stacked, index):
    return lax.dynamic_index_in_dim(stacked, index, 0, keepdims=False)


def total(terms):
    out = terms[0].astype(F32)
    for term in terms[1:]:
        out = out + term.astype(F32)
    return out


def swap_xz(v):
    return lax.ppermute(v, ("x", "z"), [(4 * i + j, 4 * j + i) for i in range(4) for j in range(4)])


def softplus(v):
    return jnp.maximum(v, 0.0) + jnp.log1p(jnp.exp(-jnp.abs(v)))


def silu(v):
    return v / (1.0 + jnp.exp(-v))


def state_kernel(maps_ref, low_ref, weight_ref, bias_ref, mixed_ref, rate_ref, *refs):
    step_ref, drive_ref, out_ref = refs[-3:]
    steps, states = step_ref.shape[0], rate_ref.shape[0]
    lanes = step_ref.shape[2]
    for pair in range(4):
        at = slice(2 * pair * lanes, 2 * (pair + 1) * lanes)
        step = softplus(jnp.dot(low_ref[...], weight_ref[:, at], preferred_element_type=F32) + bias_ref[:, at])
        drive = step * mixed_ref[:, at]
        for side in range(2):
            part = slice(side * lanes, (side + 1) * lanes)
            step_ref[:, 2 * pair + side, :] = step[:, part]
            drive_ref[:, 2 * pair + side, :] = drive[:, part]
    rates = [rate_ref[n] for n in range(states)]

    def body(t, carry):
        h, acc = carry
        st, du = step_ref[t], drive_ref[t]
        h = tuple(
            h[n] * jnp.exp2(st * rates[n]) + du * maps_ref[t * 2 * states + n] for n in range(states)
        )
        return h, acc + st

    zero = jnp.zeros(step_ref.shape[1:], F32)
    h, acc = lax.fori_loop(0, steps, body, ((zero,) * states, zero), unroll=2)
    for n in range(states):
        out_ref[n] = h[n].astype(BF)
    high = acc.astype(BF)
    out_ref[states] = high
    out_ref[states + 1] = (acc - high.astype(F32)).astype(BF)


def scan_kernel(
    place_ref, maps_ref, step_ref, drive_ref, rate_ref, same_ref, other_ref, mixed_ref, skip_ref, scale_ref, *refs
):
    gate_refs, out_ref, rows = refs[:4], refs[4], refs[5]
    steps, states = step_ref.shape[0], rate_ref.shape[0]
    lanes = step_ref.shape[2]
    rates = [rate_ref[n] for n in range(states)]
    x, core = place_ref[0], place_ref[1]
    section = 2 * x + core
    zero = jnp.zeros(step_ref.shape[1:], F32)

    def join(earlier, h):
        slot = lax.rem(x - earlier // 2 + 4, 4)
        mine = lax.rem(earlier, 2) == core

        def entry(n):
            return jnp.where(mine, same_ref[slot, n].astype(F32), other_ref[slot, n].astype(F32))

        acc = entry(states) + entry(states + 1)
        return tuple(h[n] * jnp.exp2(acc * rates[n]) + entry(n) for n in range(states))

    h = lax.fori_loop(0, section, join, (zero,) * states)

    def body(t, h):
        st, du = step_ref[t], drive_ref[t]
        base = t * 2 * states
        h = tuple(h[n] * jnp.exp2(st * rates[n]) + du * maps_ref[base + n] for n in range(states))
        terms = [h[n] * maps_ref[base + states + n] for n in range(states)]
        while len(terms) > 1:
            terms = [a + b for a, b in zip(terms[::2], terms[1::2])]
        rows[t] = terms[0]
        return h

    lax.fori_loop(0, steps, body, h, unroll=2)
    for j in range(8):
        at = slice(j * lanes, (j + 1) * lanes)
        gate = total([r[:, at] for r in gate_refs]) * scale_ref[...]
        out_ref[:, at] = ((rows[:, j, :] + skip_ref[:, at] * mixed_ref[:, at]) * silu(gate)).astype(BF)


def local_state(maps, low, weight, bias, mixed, rate):
    states, _, lanes = rate.shape
    steps = low.shape[0]
    return pl.pallas_call(
        state_kernel,
        out_shape=[jax.ShapeDtypeStruct((steps, 8, lanes), F32)] * 2
        + [jax.ShapeDtypeStruct((states + 2, 8, lanes), BF)],
        in_specs=[pl.BlockSpec(memory_space=pltpu.SMEM)]
        + [pl.BlockSpec(memory_space=pltpu.VMEM)] * 5,
        out_specs=[pl.BlockSpec(memory_space=pltpu.VMEM)] * 3,
        compiler_params=pltpu.CompilerParams(vmem_limit_bytes=16 * 1024 * 1024),
        name="local_state",
    )(maps, low, weight, bias.reshape(1, -1), mixed, rate)


def full_scan(place, maps, step, drive, rate, same, other, mixed, skip, scale, gates):
    return pl.pallas_call(
        scan_kernel,
        out_shape=jax.ShapeDtypeStruct(mixed.shape, BF),
        in_specs=[pl.BlockSpec(memory_space=pltpu.SMEM)] * 2 + [pl.BlockSpec(memory_space=pltpu.VMEM)] * 12,
        out_specs=pl.BlockSpec(memory_space=pltpu.VMEM),
        scratch_shapes=[pltpu.VMEM(step.shape, F32)],
        compiler_params=pltpu.CompilerParams(vmem_limit_bytes=16 * 1024 * 1024),
        name="full_scan",
    )(place, maps, step, drive, rate, same, other, mixed, skip.reshape(1, -1), scale, *gates)


def input_kernel(place_ref, inverse_ref, *refs):
    blocks, (near, far), outs, rows = refs[:4], refs[4:6], refs[6:10], refs[10]
    x, core, z = (place_ref[i] for i in range(3))
    ext = blocks[0].shape[0]
    main = ext - HALO
    half = near.shape[0]
    chunks = []
    for k in range(4):
        rows[k * ext : k * ext + main] = blocks[k][:main]
        before = jnp.where(lax.rem(z - k + 4, 4) == 0, 0.0, blocks[(k + 1) % 4][main:].astype(F32))
        halo = jnp.where(core == 1, blocks[k][main:].astype(F32), before)
        rows[k * ext + main : (k + 1) * ext] = halo.astype(BF)
        chunks.append(lax.rem(z - x - k + 8, 4))
    tile = 256
    for n in range(near.shape[1] // tile):
        at = slice(n * tile, (n + 1) * tile)
        out = jnp.dot(rows[:, :half], near[:, at], preferred_element_type=F32)
        out = out + jnp.dot(rows[:, half:], far[:, at], preferred_element_type=F32)
        for k in range(4):
            top, low = out[k * ext : k * ext + main].astype(BF), out[k * ext + main : (k + 1) * ext]
            if n == 0:
                raw = rows[k * ext : (k + 1) * ext].astype(F32) * inverse_ref[...]
                square = jnp.broadcast_to(jnp.sum(raw * raw, axis=1, keepdims=True), (ext, main))
                last = jnp.concatenate([square[main:], jnp.zeros((main - HALO, main), F32)], axis=0)
                row = jnp.concatenate([square[:main].T[:HALO], last.T[:HALO]], axis=1)
                high = row.astype(BF).astype(F32)
                which = lax.broadcasted_iota(jnp.int32, low.shape, 0)
                low = jnp.where(which == 0, high, jnp.where(which == 1, row - high, low))
            low = low.astype(BF)
            for m in range(4):

                @pl.when(chunks[k] == m)
                def _():
                    outs[m][:main, at] = top
                    outs[m][main:, at] = low


def input_product(place, inverse, blocks, near, far):
    ext, wide = blocks[0].shape
    return pl.pallas_call(
        input_kernel,
        out_shape=[jax.ShapeDtypeStruct((ext, near.shape[1]), BF)] * 4,
        in_specs=[pl.BlockSpec(memory_space=pltpu.SMEM)] + [pl.BlockSpec(memory_space=pltpu.VMEM)] * 7,
        out_specs=[pl.BlockSpec(memory_space=pltpu.VMEM)] * 4,
        scratch_shapes=[pltpu.VMEM((4 * ext, wide), BF)],
        compiler_params=pltpu.CompilerParams(vmem_limit_bytes=16 * 1024 * 1024),
        name="input_product",
    )(place, inverse.reshape(1, -1), *blocks, near, far)


def gate_kernel(place_ref, after_ref, *refs):
    blocks, (near, far), outs, rows = refs[:4], refs[4:6], refs[6:10], refs[10]
    x, z = place_ref[0], place_ref[2]
    main, half = outs[0].shape[0], near.shape[0]
    for k in range(4):
        rows[k * main : (k + 1) * main] = blocks[k][:main]
    tile = 256
    for n in range(near.shape[1] // tile):
        at = slice(n * tile, (n + 1) * tile)
        out = jnp.dot(rows[:, :half], near[:, at], preferred_element_type=F32)
        out = (out + jnp.dot(rows[:, half:], far[:, at], preferred_element_type=F32)).astype(BF)
        for k in range(4):
            chunk = lax.rem(z - x - k + 8, 4)
            for m in range(4):

                @pl.when(chunk == m)
                def _():
                    outs[m][:, at] = out[k * main : (k + 1) * main]


def gate_product(place, after, blocks, near, far):
    ext, wide = blocks[0].shape
    main = ext - HALO
    return pl.pallas_call(
        gate_kernel,
        out_shape=[jax.ShapeDtypeStruct((main, near.shape[1]), BF)] * 4,
        in_specs=[pl.BlockSpec(memory_space=pltpu.SMEM), pl.BlockSpec(memory_space=pl.ANY)]
        + [pl.BlockSpec(memory_space=pltpu.VMEM)] * 6,
        out_specs=[pl.BlockSpec(memory_space=pltpu.VMEM)] * 4,
        scratch_shapes=[pltpu.VMEM((4 * main, wide), BF)],
        compiler_params=pltpu.CompilerParams(vmem_limit_bytes=16 * 1024 * 1024),
        cost_estimate=pl.CostEstimate(flops=8 * main * wide * near.shape[1], bytes_accessed=6 * 2**20, transcendentals=0),
        name="gate_product",
    )(place, after, *blocks, near, far)


def sum_kernel(*refs):
    refs[-1][...] = total([r[...] for r in refs[:4]]).astype(BF)


def sum_after(blocks, after):
    return pl.pallas_call(
        sum_kernel,
        out_shape=jax.ShapeDtypeStruct(blocks[0].shape, BF),
        in_specs=[pl.BlockSpec(memory_space=pltpu.VMEM)] * 4 + [pl.BlockSpec(memory_space=pl.ANY)] * len(after),
        out_specs=pl.BlockSpec(memory_space=pltpu.VMEM),
        name="sum_after",
    )(*blocks, *after)


def stack_kernel(*refs):
    for k in range(4):
        refs[8][k] = refs[k][...]
        refs[9][k] = refs[4 + k][...]


def stack_pair(first, second):
    return pl.pallas_call(
        stack_kernel,
        out_shape=[jax.ShapeDtypeStruct((4,) + v[0].shape, BF) for v in (first, second)],
        in_specs=[pl.BlockSpec(memory_space=pltpu.VMEM)] * 8,
        out_specs=[pl.BlockSpec(memory_space=pltpu.VMEM)] * 2,
        name="stack_pair",
    )(*first, *second)


def scatter_sum(blocks, axis, sign):
    return total([blocks[0]] + [shift(blocks[k], axis, sign * k % 4) for k in range(1, 4)])


def load_kernel(after_ref, *refs):
    sources, targets, sem = refs[:3], refs[3:6], refs[6]
    copies = [pltpu.make_async_copy(s, t, sem.at[n]) for n, (s, t) in enumerate(zip(sources, targets))]
    for copy in copies:
        copy.start()
    for copy in copies:
        copy.wait()


def load_weights(after, *weights):
    return pl.pallas_call(
        load_kernel,
        out_shape=[jax.ShapeDtypeStruct(w.shape, w.dtype) for w in weights],
        in_specs=[pl.BlockSpec(memory_space=pl.ANY)] * 4,
        out_specs=[pl.BlockSpec(memory_space=pltpu.VMEM)] * 3,
        scratch_shapes=[pltpu.SemaphoreType.DMA((3,))],
        compiler_params=pltpu.CompilerParams(vmem_limit_bytes=24 * 1024 * 1024),
        cost_estimate=pl.CostEstimate(flops=0, bytes_accessed=2 * sum(w.size * 2 for w in weights), transcendentals=0),
        name="load_weights",
    )(after, *weights)


def expert_kernel(place_ref, gain_ref, *refs):
    first, second, (gate_ref, up_ref, down_ref) = refs[:4], refs[4:8], refs[8:11]
    first_out, second_out, (batch, active) = refs[11:15], refs[15:19], refs[19:]
    _, count, wide = first[0].shape
    share = wide // 4
    width = batch.shape[1]
    x, y = place_ref[0], place_ref[3]

    def column(i, j):
        return pl.multiple_of(lax.rem(x - i + 4, 4) * wide + lax.rem(y - j + 4, 4) * share, share)

    for half, source in enumerate((first, second)):
        for k in range(4):
            blocks = [(source[k][j] if half == 0 else source[j][k]).astype(F32) for j in range(4)]
            square = sum(jnp.sum(b * b, axis=1, keepdims=True) for b in blocks)
            scale = lax.rsqrt(square / width + EPS)
            top = (half * 4 + k) * count
            for j in range(4):
                for i in range(4):
                    at = pl.ds(column(i, j), share)
                    piece = blocks[j][:, i * share : (i + 1) * share] * scale * gain_ref[:, at]
                    batch[top : top + count, at] = piece.astype(BF)
    for number in range(active.shape[1] // share):
        at = slice(number * share, (number + 1) * share)
        gate = jnp.dot(batch[...], gate_ref[:, at], preferred_element_type=F32)
        up = jnp.dot(batch[...], up_ref[:, at], preferred_element_type=F32)
        active[:, at] = (silu(gate) * up).astype(BF)
    for j in range(4):
        for i in range(4):
            out = jnp.dot(active[...], down_ref[:, pl.ds(column(i, j), share)], preferred_element_type=F32).astype(BF)
            at = slice(i * share, (i + 1) * share)
            for k in range(4):
                first_out[k][j, :, at] = out[k * count : (k + 1) * count]
                second_out[j][k, :, at] = out[(4 + k) * count : (5 + k) * count]


def expert_block(place, gain, first, second, w_gate, w_up, w_down):
    width, hidden = w_gate.shape
    _, count, wide = first[0].shape
    out = pl.pallas_call(
        expert_kernel,
        out_shape=[jax.ShapeDtypeStruct((4, count, wide), BF)] * 8,
        in_specs=[pl.BlockSpec(memory_space=pltpu.SMEM)] + [pl.BlockSpec(memory_space=pltpu.VMEM)] * 12,
        out_specs=[pl.BlockSpec(memory_space=pltpu.VMEM)] * 8,
        scratch_shapes=[pltpu.VMEM((8 * count, width), BF), pltpu.VMEM((8 * count, hidden), BF)],
        compiler_params=pltpu.CompilerParams(vmem_limit_bytes=12 * 1024 * 1024),
        cost_estimate=pl.CostEstimate(
            flops=48 * count * width * hidden, bytes_accessed=6 * width * hidden, transcendentals=8 * count * hidden
        ),
        name="expert_block",
    )(place, gain.reshape(1, -1), *first, *second, w_gate, w_up, w_down)
    return out[:4], out[4:]


def shards(
    tokens,
    norm_gain,
    in_x,
    in_z,
    conv_weight,
    conv_bias,
    xproj_weight,
    dt_weight,
    dt_bias,
    a_log,
    skip_d,
    out_weight,
    moe_gain,
    expert_ids,
    route_gates,
    w_gate,
    w_up,
    w_down,
):
    x, core, z, y = (lax.axis_index(a) for a in ("x", "core", "z", "y"))
    block_rows, col_share = tokens.shape
    width = norm_gain.shape[0]
    channels = in_x.shape[1]
    lanes = channels // 8
    rank = dt_weight.shape[0]
    states = a_log.shape[1]
    swap_cores = [(0, 1), (1, 0)]

    place = jnp.stack([x, core, z, y]).astype(jnp.int32)

    own = swap_xz(tokens)
    tail = lax.ppermute(own[block_rows - HALO :], "core", swap_cores)
    gains = lax.dynamic_slice_in_dim(norm_gain, x * 4 * col_share, 4 * col_share).reshape(4, col_share)
    gained = (jnp.concatenate([own, tail], axis=0).astype(F32) * pick(gains, y)).astype(BF)

    order = [(2 * core + i) % 4 for i in range(4)]
    parts = jnp.stack(gather_rel(gained, "y"))
    wide = jnp.concatenate([pick(parts, (y - o + 4) % 4) for o in order], axis=1)
    blocks = gather_rel(wide, "z")
    far_x = lax.ppermute(in_x, "core", swap_cores)
    far_z = lax.ppermute(in_z, "core", swap_cores)
    inverse = 1.0 / jnp.concatenate([pick(gains, o) for o in order])
    part_u = input_product(place, inverse, blocks, in_x, far_x)
    sum_u = scatter_sum(part_u, "x", 1)
    mean_sq = (sum_u[block_rows] + sum_u[block_rows + 1]) / width
    scale = lax.rsqrt(mean_sq[: block_rows + HALO] + EPS)[:, None]
    inner_u = sum_u * scale

    taps = conv_weight.shape[0]
    inner_u = jnp.concatenate([inner_u[block_rows + HALO - (taps - 1) :], inner_u[:block_rows]], axis=0)
    conv_sum = conv_bias + jnp.zeros((block_rows, channels), F32)
    for offset in range(taps):
        conv_sum = conv_sum + conv_weight[offset] * inner_u[offset : offset + block_rows]
    mixed_in = silu(conv_sum)

    part_p = jnp.dot(mixed_in.astype(BF), xproj_weight, preferred_element_type=F32).astype(BF)
    gate_raw = gate_product(place, part_u[0], blocks, in_z, far_z)
    gate_parts = [gate_raw[0]] + [shift(gate_raw[d], "x", d) for d in range(1, 4)]
    projected = sum_after(gather_rel(part_p, "y"), gate_parts[1:])
    projected = total(gather_rel(projected, "z")).astype(BF)

    dt_low = projected[:, :rank]
    maps = projected[:, rank:].astype(F32).reshape(-1)
    rate = (-jnp.exp(a_log) * LOG2E).T.reshape(states, 8, lanes)
    step, drive, ends = local_state(maps, dt_low, dt_weight, dt_bias, mixed_in, rate)
    same = jnp.stack(gather_rel(ends, "x"))
    other = lax.ppermute(same, "core", swap_cores)
    gated = full_scan(
        place, maps, step, drive, rate, same, other, mixed_in, skip_d, scale[:block_rows], gate_parts
    )

    far_out = lax.ppermute(out_weight, "core", swap_cores)
    out_both = jnp.where(
        core == 0,
        jnp.concatenate([out_weight, far_out], axis=1),
        jnp.concatenate([far_out, out_weight], axis=1),
    )
    gated_rows = jnp.concatenate(gather_rel(gated, "x"), axis=0)
    part_o = jnp.dot(gated_rows, out_both, preferred_element_type=F32).astype(BF).reshape(4, block_rows, -1)
    sum_o = scatter_sum([pick(part_o, (x - z - d + 8) % 4) for d in range(4)], "z", 1).astype(BF)
    sum_o = sum_o.reshape(block_rows, 4, col_share).transpose(1, 0, 2)
    mixer = scatter_sum([pick(sum_o, (y + d) % 4) for d in range(4)], "y", 1)
    resid = (own.astype(F32) + mixer).astype(BF)

    top = expert_ids.shape[1]
    experts = lax.axis_size("x") * lax.axis_size("core")
    capacity = block_rows * top * 3 // (2 * experts)
    flat = jnp.arange(block_rows * top, dtype=jnp.int32)
    before = (flat[:, None] > flat[None, :]).astype(BF)

    def slots(ids):
        one_hot = ids[:, None] == jnp.arange(experts, dtype=jnp.int32)[None, :]
        earlier = jnp.dot(before, one_hot.astype(BF), preferred_element_type=F32)
        return ids * capacity + jnp.sum(jnp.where(one_hot, earlier, 0.0), axis=1).astype(jnp.int32)

    routing = swap_xz(jnp.concatenate([expert_ids.astype(F32).T, route_gates.T], axis=0))
    gates = routing[top:]
    named = jnp.stack([2 * ((x + d) % 4) + (core + c) % 2 for c in range(2) for d in range(4)])
    cells = (named[:, None] * capacity + jnp.arange(capacity, dtype=jnp.int32)[None, :]).reshape(1, -1)
    fetch = slots(routing[:top].reshape(-1).astype(jnp.int32))[:, None] == cells
    send = (fetch[:block_rows] | fetch[block_rows:]).astype(BF)

    outgoing = lax.dot_general(send, resid, (((0,), (0,)), ((), ())), preferred_element_type=F32).astype(BF)
    outgoing = outgoing.reshape(2, 4, capacity, col_share)
    both = jnp.stack([outgoing[0], lax.ppermute(outgoing[1], "core", swap_cores)], axis=1)
    received = [both[0]] + [shift(both[d], "x", d) for d in range(1, 4)]
    halves = jnp.concatenate(received, axis=2)

    first, second = stack_pair(gather_rel(halves[0], "y"), gather_rel(halves[1], "z"))
    weights = load_weights(first, w_gate[0], w_up[0], w_down[0])
    first, second = gather_rel(first, "z"), gather_rel(second, "y")
    first, second = expert_block(place, moe_gain, first, second, *weights)
    first = scatter_sum(scatter_sum(first, "z", -1).astype(BF), "y", -1).astype(BF)
    second = scatter_sum(scatter_sum(second, "y", -1).astype(BF), "z", -1).astype(BF)
    back = jnp.stack([first, second]).reshape(2, capacity, 4, col_share).transpose(2, 0, 1, 3)
    back = [back[0]] + [shift(back[d], "x", 4 - d) for d in range(1, 4)]
    far_back = lax.ppermute(jnp.stack([b[1] for b in back]), "core", swap_cores)
    returned = jnp.concatenate([b[0] for b in back] + [far_back.reshape(4 * capacity, col_share)], axis=0)
    picked = jnp.dot(fetch.astype(BF), returned, preferred_element_type=F32)
    moe = picked[:block_rows] * gates[0][:, None] + picked[block_rows:] * gates[1][:, None]
    return swap_xz((resid.astype(F32) + moe).astype(BF))


def solution(mesh):
    fine = Mesh(mesh.devices.reshape(4, 2, 4, 4), ("x", "core", "z", "y"))
    section, tp = ("x", "core"), ("z", "y")
    placed = (
        P(section, tp),
        P(),
        P(section, tp),
        P(section, tp),
        P(None, tp),
        P(tp),
        P(tp, None),
        P(None, tp),
        P(tp),
        P(tp, None),
        P(tp),
        P(tp, section),
        P(),
        P(section, None),
        P(section, None),
        P(section, None, tp),
        P(section, None, tp),
        P(section, tp, None),
    )
    return jax.shard_map(
        shards, mesh=fine, in_specs=placed, out_specs=P(section, tp), check_vma=False
    )
```

```python
import jax
import jax.numpy as jnp
from jax import lax
from jax.experimental import pallas as pl
from jax.experimental.pallas import tpu as pltpu
from jax.sharding import Mesh, PartitionSpec as P

EPS = 1e-05
BF = jnp.bfloat16
F32 = jnp.float32
LOG2E = 1.4426950408889634
HALO = 16


def shift(v, axis, d):
    n = lax.axis_size(axis)
    return lax.ppermute(v, axis, [(i, (i + d) % n) for i in range(n)])


def gather_rel(v, axis):
    return [v] + [shift(v, axis, d) for d in range(1, lax.axis_size(axis))]


def pick(stacked, index):
    return lax.dynamic_index_in_dim(stacked, index, 0, keepdims=False)


def total(terms):
    out = terms[0].astype(F32)
    for term in terms[1:]:
        out = out + term.astype(F32)
    return out


def swap_xz(v):
    return lax.ppermute(v, ("x", "z"), [(4 * i + j, 4 * j + i) for i in range(4) for j in range(4)])


def softplus(v):
    return jnp.maximum(v, 0.0) + jnp.log1p(jnp.exp(-jnp.abs(v)))


def silu(v):
    return v / (1.0 + jnp.exp(-v))


def state_kernel(maps_ref, low_ref, weight_ref, bias_ref, mixed_ref, rate_ref, *refs):
    step_ref, drive_ref, out_ref = refs[-3:]
    steps, states = step_ref.shape[0], rate_ref.shape[0]
    lanes = step_ref.shape[2]
    for pair in range(4):
        at = slice(2 * pair * lanes, 2 * (pair + 1) * lanes)
        step = softplus(jnp.dot(low_ref[...], weight_ref[:, at], preferred_element_type=F32) + bias_ref[:, at])
        drive = step * mixed_ref[:, at]
        for side in range(2):
            part = slice(side * lanes, (side + 1) * lanes)
            step_ref[:, 2 * pair + side, :] = step[:, part]
            drive_ref[:, 2 * pair + side, :] = drive[:, part]
    rates = [rate_ref[n] for n in range(states)]

    def body(t, carry):
        h, acc = carry
        st, du = step_ref[t], drive_ref[t]
        h = tuple(
            h[n] * jnp.exp2(st * rates[n]) + du * maps_ref[t * 2 * states + n] for n in range(states)
        )
        return h, acc + st

    zero = jnp.zeros(step_ref.shape[1:], F32)
    h, acc = lax.fori_loop(0, steps, body, ((zero,) * states, zero), unroll=2)
    for n in range(states):
        out_ref[n] = h[n].astype(BF)
    high = acc.astype(BF)
    out_ref[states] = high
    out_ref[states + 1] = (acc - high.astype(F32)).astype(BF)


def scan_kernel(
    place_ref, maps_ref, step_ref, drive_ref, rate_ref, same_ref, other_ref, mixed_ref, skip_ref, scale_ref, *refs
):
    gate_refs, out_ref, rows = refs[:4], refs[4], refs[5]
    steps, states = step_ref.shape[0], rate_ref.shape[0]
    lanes = step_ref.shape[2]
    rates = [rate_ref[n] for n in range(states)]
    x, core = place_ref[0], place_ref[1]
    section = 2 * x + core
    zero = jnp.zeros(step_ref.shape[1:], F32)

    def join(earlier, h):
        slot = lax.rem(x - earlier // 2 + 4, 4)
        mine = lax.rem(earlier, 2) == core

        def entry(n):
            return jnp.where(mine, same_ref[slot, n].astype(F32), other_ref[slot, n].astype(F32))

        acc = entry(states) + entry(states + 1)
        return tuple(h[n] * jnp.exp2(acc * rates[n]) + entry(n) for n in range(states))

    h = lax.fori_loop(0, section, join, (zero,) * states)

    def body(t, h):
        st, du = step_ref[t], drive_ref[t]
        base = t * 2 * states
        h = tuple(h[n] * jnp.exp2(st * rates[n]) + du * maps_ref[base + n] for n in range(states))
        terms = [h[n] * maps_ref[base + states + n] for n in range(states)]
        while len(terms) > 1:
            terms = [a + b for a, b in zip(terms[::2], terms[1::2])]
        rows[t] = terms[0]
        return h

    lax.fori_loop(0, steps, body, h, unroll=2)
    for j in range(8):
        at = slice(j * lanes, (j + 1) * lanes)
        gate = total([r[:, at] for r in gate_refs]) * scale_ref[...]
        out_ref[:, at] = ((rows[:, j, :] + skip_ref[:, at] * mixed_ref[:, at]) * silu(gate)).astype(BF)


def local_state(maps, low, weight, bias, mixed, rate):
    states, _, lanes = rate.shape
    steps = low.shape[0]
    return pl.pallas_call(
        state_kernel,
        out_shape=[jax.ShapeDtypeStruct((steps, 8, lanes), F32)] * 2
        + [jax.ShapeDtypeStruct((states + 2, 8, lanes), BF)],
        in_specs=[pl.BlockSpec(memory_space=pltpu.SMEM)]
        + [pl.BlockSpec(memory_space=pltpu.VMEM)] * 5,
        out_specs=[pl.BlockSpec(memory_space=pltpu.VMEM)] * 3,
        compiler_params=pltpu.CompilerParams(vmem_limit_bytes=16 * 1024 * 1024),
        name="local_state",
    )(maps, low, weight, bias.reshape(1, -1), mixed, rate)


def full_scan(place, maps, step, drive, rate, same, other, mixed, skip, scale, gates):
    return pl.pallas_call(
        scan_kernel,
        out_shape=jax.ShapeDtypeStruct(mixed.shape, BF),
        in_specs=[pl.BlockSpec(memory_space=pltpu.SMEM)] * 2 + [pl.BlockSpec(memory_space=pltpu.VMEM)] * 12,
        out_specs=pl.BlockSpec(memory_space=pltpu.VMEM),
        scratch_shapes=[pltpu.VMEM(step.shape, F32)],
        compiler_params=pltpu.CompilerParams(vmem_limit_bytes=16 * 1024 * 1024),
        name="full_scan",
    )(place, maps, step, drive, rate, same, other, mixed, skip.reshape(1, -1), scale, *gates)


def input_kernel(place_ref, inverse_ref, *refs):
    blocks, (near, far), outs, rows = refs[:4], refs[4:6], refs[6:10], refs[10]
    x, core, z = (place_ref[i] for i in range(3))
    ext = blocks[0].shape[0]
    main = ext - HALO
    half = near.shape[0]
    chunks = []
    for k in range(4):
        rows[k * ext : k * ext + main] = blocks[k][:main]
        before = jnp.where(lax.rem(z - k + 4, 4) == 0, 0.0, blocks[(k + 1) % 4][main:].astype(F32))
        halo = jnp.where(core == 1, blocks[k][main:].astype(F32), before)
        rows[k * ext + main : (k + 1) * ext] = halo.astype(BF)
        chunks.append(lax.rem(z - x - k + 8, 4))
    tile = 256
    for n in range(near.shape[1] // tile):
        at = slice(n * tile, (n + 1) * tile)
        out = jnp.dot(rows[:, :half], near[:, at], preferred_element_type=F32)
        out = out + jnp.dot(rows[:, half:], far[:, at], preferred_element_type=F32)
        for k in range(4):
            top, low = out[k * ext : k * ext + main].astype(BF), out[k * ext + main : (k + 1) * ext]
            if n == 0:
                raw = rows[k * ext : (k + 1) * ext].astype(F32) * inverse_ref[...]
                square = jnp.broadcast_to(jnp.sum(raw * raw, axis=1, keepdims=True), (ext, main))
                last = jnp.concatenate([square[main:], jnp.zeros((main - HALO, main), F32)], axis=0)
                row = jnp.concatenate([square[:main].T[:HALO], last.T[:HALO]], axis=1)
                high = row.astype(BF).astype(F32)
                which = lax.broadcasted_iota(jnp.int32, low.shape, 0)
                low = jnp.where(which == 0, high, jnp.where(which == 1, row - high, low))
            low = low.astype(BF)
            for m in range(4):

                @pl.when(chunks[k] == m)
                def _():
                    outs[m][:main, at] = top
                    outs[m][main:, at] = low


def input_product(place, inverse, blocks, near, far):
    ext, wide = blocks[0].shape
    return pl.pallas_call(
        input_kernel,
        out_shape=[jax.ShapeDtypeStruct((ext, near.shape[1]), BF)] * 4,
        in_specs=[pl.BlockSpec(memory_space=pltpu.SMEM)] + [pl.BlockSpec(memory_space=pltpu.VMEM)] * 7,
        out_specs=[pl.BlockSpec(memory_space=pltpu.VMEM)] * 4,
        scratch_shapes=[pltpu.VMEM((4 * ext, wide), BF)],
        compiler_params=pltpu.CompilerParams(vmem_limit_bytes=16 * 1024 * 1024),
        name="input_product",
    )(place, inverse.reshape(1, -1), *blocks, near, far)


def gate_kernel(place_ref, after_ref, *refs):
    blocks, (near, far), outs, rows = refs[:4], refs[4:6], refs[6:10], refs[10]
    x, z = place_ref[0], place_ref[2]
    main, half = outs[0].shape[0], near.shape[0]
    for k in range(4):
        rows[k * main : (k + 1) * main] = blocks[k][:main]
    tile = 256
    for n in range(near.shape[1] // tile):
        at = slice(n * tile, (n + 1) * tile)
        out = jnp.dot(rows[:, :half], near[:, at], preferred_element_type=F32)
        out = (out + jnp.dot(rows[:, half:], far[:, at], preferred_element_type=F32)).astype(BF)
        for k in range(4):
            chunk = lax.rem(z - x - k + 8, 4)
            for m in range(4):

                @pl.when(chunk == m)
                def _():
                    outs[m][:, at] = out[k * main : (k + 1) * main]


def gate_product(place, after, blocks, near, far):
    ext, wide = blocks[0].shape
    main = ext - HALO
    return pl.pallas_call(
        gate_kernel,
        out_shape=[jax.ShapeDtypeStruct((main, near.shape[1]), BF)] * 4,
        in_specs=[pl.BlockSpec(memory_space=pltpu.SMEM), pl.BlockSpec(memory_space=pl.ANY)]
        + [pl.BlockSpec(memory_space=pltpu.VMEM)] * 6,
        out_specs=[pl.BlockSpec(memory_space=pltpu.VMEM)] * 4,
        scratch_shapes=[pltpu.VMEM((4 * main, wide), BF)],
        compiler_params=pltpu.CompilerParams(vmem_limit_bytes=16 * 1024 * 1024),
        cost_estimate=pl.CostEstimate(flops=8 * main * wide * near.shape[1], bytes_accessed=6 * 2**20, transcendentals=0),
        name="gate_product",
    )(place, after, *blocks, near, far)


def sum_kernel(*refs):
    refs[-1][...] = total([r[...] for r in refs[:4]]).astype(BF)


def sum_after(blocks, after):
    return pl.pallas_call(
        sum_kernel,
        out_shape=jax.ShapeDtypeStruct(blocks[0].shape, BF),
        in_specs=[pl.BlockSpec(memory_space=pltpu.VMEM)] * 4 + [pl.BlockSpec(memory_space=pl.ANY)] * len(after),
        out_specs=pl.BlockSpec(memory_space=pltpu.VMEM),
        name="sum_after",
    )(*blocks, *after)


def beside_kernel(*refs):
    for k in range(4):
        refs[5][k] = total([r[k] for r in refs[:4]]).astype(BF)
    refs[6][...] = refs[4][...]


def sum_beside(blocks, rows):
    return pl.pallas_call(
        beside_kernel,
        out_shape=[jax.ShapeDtypeStruct(v.shape, BF) for v in (blocks[0], rows)],
        in_specs=[pl.BlockSpec(memory_space=pltpu.VMEM)] * 5,
        out_specs=[pl.BlockSpec(memory_space=pltpu.VMEM)] * 2,
        name="sum_beside",
    )(*blocks, rows)


def stack_kernel(*refs):
    for k in range(4):
        refs[8][k] = refs[k][...]
        refs[9][k] = refs[4 + k][...]


def stack_pair(first, second):
    return pl.pallas_call(
        stack_kernel,
        out_shape=[jax.ShapeDtypeStruct((4,) + v[0].shape, BF) for v in (first, second)],
        in_specs=[pl.BlockSpec(memory_space=pltpu.VMEM)] * 8,
        out_specs=[pl.BlockSpec(memory_space=pltpu.VMEM)] * 2,
        name="stack_pair",
    )(*first, *second)


def scatter_sum(blocks, axis, sign):
    return total([blocks[0]] + [shift(blocks[k], axis, sign * k % 4) for k in range(1, 4)])


def load_kernel(*refs):
    sources, targets, sem = refs[:3], refs[-4:-1], refs[-1]
    copies = [pltpu.make_async_copy(s, t, sem.at[n]) for n, (s, t) in enumerate(zip(sources, targets))]
    for copy in copies:
        copy.start()
    for copy in copies:
        copy.wait()


def load_weights(weights, after):
    return pl.pallas_call(
        load_kernel,
        out_shape=[jax.ShapeDtypeStruct(w.shape, w.dtype) for w in weights],
        in_specs=[pl.BlockSpec(memory_space=pl.ANY)] * (3 + len(after)),
        out_specs=[pl.BlockSpec(memory_space=pltpu.VMEM)] * 3,
        scratch_shapes=[pltpu.SemaphoreType.DMA((3,))],
        compiler_params=pltpu.CompilerParams(vmem_limit_bytes=24 * 1024 * 1024),
        cost_estimate=pl.CostEstimate(flops=0, bytes_accessed=2 * sum(w.size * 2 for w in weights), transcendentals=0),
        name="load_weights",
    )(*weights, *after)


def expert_kernel(place_ref, gain_ref, *refs):
    first, second, (gate_ref, up_ref, down_ref) = refs[:4], refs[4:8], refs[8:11]
    first_out, second_out, (batch, active) = refs[11:15], refs[15:19], refs[19:]
    _, count, wide = first[0].shape
    share = wide // 4
    width = batch.shape[1]
    x, z, y = place_ref[0], place_ref[2], place_ref[3]

    def column(i, j):
        return pl.multiple_of(lax.rem(x - i + 4, 4) * wide + lax.rem(y - j + 4, 4) * share, share)

    for half, source in enumerate((first, second)):
        for k in range(4):
            blocks = [(source[k][j] if half == 0 else source[j][k]).astype(F32) for j in range(4)]
            square = sum(jnp.sum(b * b, axis=1, keepdims=True) for b in blocks)
            scale = lax.rsqrt(square / width + EPS)
            top = pl.ds(pl.multiple_of((half * 4 + lax.rem(z - k - x + 8, 4)) * count, 16), count)
            for j in range(4):
                for i in range(4):
                    at = pl.ds(column(i, j), share)
                    piece = blocks[j][:, i * share : (i + 1) * share] * scale * gain_ref[:, at]
                    batch[top, at] = piece.astype(BF)
    for number in range(active.shape[1] // share):
        at = slice(number * share, (number + 1) * share)
        gate = jnp.dot(batch[...], gate_ref[:, at], preferred_element_type=F32)
        up = jnp.dot(batch[...], up_ref[:, at], preferred_element_type=F32)
        active[:, at] = (silu(gate) * up).astype(BF)
    for k in range(4):
        for j in range(4):
            column_out = lax.rem(z - k + 4, 4) * wide + lax.rem(y - j + 4, 4) * share
            at = pl.ds(pl.multiple_of(column_out, share), share)
            out = jnp.dot(active[...], down_ref[:, at], preferred_element_type=F32).astype(BF)
            first_out[k][j] = out[: 4 * count]
            second_out[j][k] = out[4 * count :]


def expert_block(place, gain, first, second, w_gate, w_up, w_down):
    width, hidden = w_gate.shape
    _, count, wide = first[0].shape
    out = pl.pallas_call(
        expert_kernel,
        out_shape=[jax.ShapeDtypeStruct((4, 4 * count, wide // 4), BF)] * 8,
        in_specs=[pl.BlockSpec(memory_space=pltpu.SMEM)] + [pl.BlockSpec(memory_space=pltpu.VMEM)] * 12,
        out_specs=[pl.BlockSpec(memory_space=pltpu.VMEM)] * 8,
        scratch_shapes=[pltpu.VMEM((8 * count, width), BF), pltpu.VMEM((8 * count, hidden), BF)],
        compiler_params=pltpu.CompilerParams(vmem_limit_bytes=12 * 1024 * 1024),
        cost_estimate=pl.CostEstimate(
            flops=48 * count * width * hidden, bytes_accessed=6 * width * hidden, transcendentals=8 * count * hidden
        ),
        name="expert_block",
    )(place, gain.reshape(1, -1), *first, *second, w_gate, w_up, w_down)
    return out[:4], out[4:]


def shards(
    tokens,
    norm_gain,
    in_x,
    in_z,
    conv_weight,
    conv_bias,
    xproj_weight,
    dt_weight,
    dt_bias,
    a_log,
    skip_d,
    out_weight,
    moe_gain,
    expert_ids,
    route_gates,
    w_gate,
    w_up,
    w_down,
):
    x, core, z, y = (lax.axis_index(a) for a in ("x", "core", "z", "y"))
    block_rows, col_share = tokens.shape
    width = norm_gain.shape[0]
    channels = in_x.shape[1]
    lanes = channels // 8
    rank = dt_weight.shape[0]
    states = a_log.shape[1]
    swap_cores = [(0, 1), (1, 0)]

    place = jnp.stack([x, core, z, y]).astype(jnp.int32)

    ids_rows = jnp.pad(expert_ids.T.astype(BF), ((0, HALO - expert_ids.shape[1]), (0, col_share - block_rows)))
    swapped = swap_xz(jnp.concatenate([tokens, ids_rows], axis=0))
    own = swapped[:block_rows]
    tail = lax.ppermute(own[block_rows - HALO :], "core", swap_cores)
    gains = lax.dynamic_slice_in_dim(norm_gain, x * 4 * col_share, 4 * col_share).reshape(4, col_share)
    gained = (jnp.concatenate([own, tail], axis=0).astype(F32) * pick(gains, y)).astype(BF)

    order = [(2 * core + i) % 4 for i in range(4)]
    parts = jnp.stack(gather_rel(gained, "y"))
    wide = jnp.concatenate([pick(parts, (y - o + 4) % 4) for o in order], axis=1)
    blocks = gather_rel(wide, "z")
    far_x = lax.ppermute(in_x, "core", swap_cores)
    far_z = lax.ppermute(in_z, "core", swap_cores)
    inverse = 1.0 / jnp.concatenate([pick(gains, o) for o in order])
    part_u = input_product(place, inverse, blocks, in_x, far_x)
    sum_u = scatter_sum(part_u, "x", 1)
    mean_sq = (sum_u[block_rows] + sum_u[block_rows + 1]) / width
    scale = lax.rsqrt(mean_sq[: block_rows + HALO] + EPS)[:, None]
    inner_u = sum_u * scale

    taps = conv_weight.shape[0]
    inner_u = jnp.concatenate([inner_u[block_rows + HALO - (taps - 1) :], inner_u[:block_rows]], axis=0)
    conv_sum = conv_bias + jnp.zeros((block_rows, channels), F32)
    for offset in range(taps):
        conv_sum = conv_sum + conv_weight[offset] * inner_u[offset : offset + block_rows]
    mixed_in = silu(conv_sum)

    part_p = jnp.dot(mixed_in.astype(BF), xproj_weight, preferred_element_type=F32).astype(BF)
    gate_raw = gate_product(place, part_u[0], blocks, in_z, far_z)
    gate_parts = [gate_raw[0]] + [shift(gate_raw[d], "x", d) for d in range(1, 4)]
    projected = sum_after(gather_rel(part_p, "y"), gate_parts[1:])
    projected = total(gather_rel(projected, "z")).astype(BF)

    dt_low = projected[:, :rank]
    maps = projected[:, rank:].astype(F32).reshape(-1)
    rate = (-jnp.exp(a_log) * LOG2E).T.reshape(states, 8, lanes)
    step, drive, ends = local_state(maps, dt_low, dt_weight, dt_bias, mixed_in, rate)
    same = jnp.stack(gather_rel(ends, "x"))
    other = lax.ppermute(same, "core", swap_cores)
    gated = full_scan(
        place, maps, step, drive, rate, same, other, mixed_in, skip_d, scale[:block_rows], gate_parts
    )

    far_out = lax.ppermute(out_weight, "core", swap_cores)
    out_both = jnp.where(
        core == 0,
        jnp.concatenate([out_weight, far_out], axis=1),
        jnp.concatenate([far_out, out_weight], axis=1),
    )
    gated_rows = jnp.concatenate(gather_rel(gated, "x"), axis=0)
    part_o = jnp.dot(gated_rows, out_both, preferred_element_type=F32).astype(BF).reshape(4, block_rows, -1)
    sum_o = scatter_sum([pick(part_o, (x - z - d + 8) % 4) for d in range(4)], "z", 1).astype(BF)
    sum_o = sum_o.reshape(block_rows, 4, col_share).transpose(1, 0, 2)
    mixer = scatter_sum([pick(sum_o, (y + d) % 4) for d in range(4)], "y", 1)
    resid = (own.astype(F32) + mixer).astype(BF)

    top = expert_ids.shape[1]
    experts = lax.axis_size("x") * lax.axis_size("core")
    capacity = block_rows * top * 3 // (2 * experts)
    flat = jnp.arange(block_rows * top, dtype=jnp.int32)
    before = (flat[:, None] > flat[None, :]).astype(BF)

    def slots(ids):
        one_hot = ids[:, None] == jnp.arange(experts, dtype=jnp.int32)[None, :]
        earlier = jnp.dot(before, one_hot.astype(BF), preferred_element_type=F32)
        return ids * capacity + jnp.sum(jnp.where(one_hot, earlier, 0.0), axis=1).astype(jnp.int32)

    def cells(sign):
        named = jnp.stack([2 * ((x + sign * d + 4) % 4) + (core + c) % 2 for c in range(2) for d in range(4)])
        return (named[:, None] * capacity + jnp.arange(capacity, dtype=jnp.int32)[None, :]).reshape(1, -1)

    away_ids = swapped[block_rows : block_rows + top, :block_rows].astype(jnp.int32).reshape(-1)
    send = slots(away_ids)[:, None] == cells(1)
    send = (send[:block_rows] | send[block_rows:]).astype(BF)
    fetch = (slots(expert_ids.T.reshape(-1))[:, None] == cells(-1)).astype(BF)

    outgoing = lax.dot_general(send, resid, (((0,), (0,)), ((), ())), preferred_element_type=F32).astype(BF)
    outgoing = outgoing.reshape(2, 4, capacity, col_share)
    both = jnp.stack([outgoing[0], lax.ppermute(outgoing[1], "core", swap_cores)], axis=1)
    received = [both[0]] + [shift(both[d], "x", d) for d in range(1, 4)]
    halves = jnp.concatenate(received, axis=2)

    first, second = stack_pair(gather_rel(halves[0], "y"), gather_rel(halves[1], "z"))
    weights = load_weights([w_gate[0], w_up[0], w_down[0]], [first])
    first, second = gather_rel(first, "z"), gather_rel(second, "y")
    first, second = expert_block(place, moe_gain, first, second, *weights)
    first = scatter_sum(scatter_sum(first, "z", -1).astype(BF), "y", -1).astype(BF)
    second, resid = sum_beside([second[0]] + [shift(second[k], "y", 4 - k) for k in range(1, 4)], resid)
    resid_home = swap_xz(resid)
    second = scatter_sum(second, "z", -1).astype(BF)
    back = jnp.stack([first.reshape(4, capacity, col_share), second.reshape(4, capacity, col_share)], axis=1)
    back = [back[0]] + [shift(back[r], "x", r) for r in range(1, 4)]
    far_back = lax.ppermute(jnp.stack([b[1] for b in back]), "core", swap_cores)
    returned = jnp.concatenate([b[0] for b in back] + [far_back.reshape(4 * capacity, col_share)], axis=0)
    picked = jnp.dot(fetch, returned, preferred_element_type=F32)
    moe = picked[:block_rows] * route_gates[:, :1] + picked[block_rows:] * route_gates[:, 1:]
    return (resid_home.astype(F32) + moe).astype(BF)


def solution(mesh):
    fine = Mesh(mesh.devices.reshape(4, 2, 4, 4), ("x", "core", "z", "y"))
    section, tp = ("x", "core"), ("z", "y")
    placed = (
        P(section, tp),
        P(),
        P(section, tp),
        P(section, tp),
        P(None, tp),
        P(tp),
        P(tp, None),
        P(None, tp),
        P(tp),
        P(tp, None),
        P(tp),
        P(tp, section),
        P(),
        P(section, None),
        P(section, None),
        P(section, None, tp),
        P(section, None, tp),
        P(section, tp, None),
    )
    return jax.shard_map(
        shards, mesh=fine, in_specs=placed, out_specs=P(section, tp), check_vma=False
    )
```

```python
import jax
import jax.numpy as jnp
from jax import lax
from jax.experimental import pallas as pl
from jax.experimental.pallas import tpu as pltpu
from jax.sharding import Mesh, PartitionSpec as P

EPS = 1e-05
BF = jnp.bfloat16
F32 = jnp.float32
LOG2E = 1.4426950408889634
HALO = 16


def shift(v, axis, d):
    n = lax.axis_size(axis)
    return lax.ppermute(v, axis, [(i, (i + d) % n) for i in range(n)])


def gather_rel(v, axis):
    return [v] + [shift(v, axis, d) for d in range(1, lax.axis_size(axis))]


def pick(stacked, index):
    return lax.dynamic_index_in_dim(stacked, index, 0, keepdims=False)


def total(terms):
    out = terms[0].astype(F32)
    for term in terms[1:]:
        out = out + term.astype(F32)
    return out


def swap_xz(v):
    return lax.ppermute(v, ("x", "z"), [(4 * i + j, 4 * j + i) for i in range(4) for j in range(4)])


def softplus(v):
    return jnp.maximum(v, 0.0) + jnp.log1p(jnp.exp(-jnp.abs(v)))


def silu(v):
    return v / (1.0 + jnp.exp(-v))


def state_kernel(maps_ref, low_ref, weight_ref, bias_ref, mixed_ref, rate_ref, *refs):
    step_ref, drive_ref, out_ref = refs[-3:]
    steps, states = step_ref.shape[0], rate_ref.shape[0]
    lanes = step_ref.shape[2]
    for pair in range(4):
        at = slice(2 * pair * lanes, 2 * (pair + 1) * lanes)
        product = lax.dot_general(
            low_ref[...], weight_ref[:, at], (((0,), (0,)), ((), ())), preferred_element_type=F32
        )
        step = softplus(product + bias_ref[:, at])
        drive = step * mixed_ref[:, at]
        for side in range(2):
            part = slice(side * lanes, (side + 1) * lanes)
            step_ref[:, 2 * pair + side, :] = step[:, part]
            drive_ref[:, 2 * pair + side, :] = drive[:, part]
    rates = [rate_ref[n] for n in range(states)]

    def body(t, carry):
        h, acc = carry
        st, du = step_ref[t], drive_ref[t]
        h = tuple(
            h[n] * jnp.exp2(st * rates[n]) + du * maps_ref[n * steps + t] for n in range(states)
        )
        return h, acc + st

    zero = jnp.zeros(step_ref.shape[1:], F32)
    h, acc = lax.fori_loop(0, steps, body, ((zero,) * states, zero), unroll=2)
    for n in range(states):
        out_ref[n] = h[n].astype(BF)
    high = acc.astype(BF)
    out_ref[states] = high
    out_ref[states + 1] = (acc - high.astype(F32)).astype(BF)


def scan_kernel(
    place_ref, maps_ref, step_ref, drive_ref, rate_ref, same_ref, other_ref, mixed_ref, skip_ref, scale_ref, *refs
):
    gate_refs, out_ref, rows = refs[:4], refs[4], refs[5]
    steps, states = step_ref.shape[0], rate_ref.shape[0]
    lanes = step_ref.shape[2]
    rates = [rate_ref[n] for n in range(states)]
    x, core = place_ref[0], place_ref[1]
    section = 2 * x + core
    zero = jnp.zeros(step_ref.shape[1:], F32)

    def join(earlier, h):
        slot = lax.rem(x - earlier // 2 + 4, 4)
        mine = lax.rem(earlier, 2) == core

        def entry(n):
            return jnp.where(mine, same_ref[slot, n].astype(F32), other_ref[slot, n].astype(F32))

        acc = entry(states) + entry(states + 1)
        return tuple(h[n] * jnp.exp2(acc * rates[n]) + entry(n) for n in range(states))

    h = lax.fori_loop(0, section, join, (zero,) * states)

    def body(t, h):
        st, du = step_ref[t], drive_ref[t]
        h = tuple(h[n] * jnp.exp2(st * rates[n]) + du * maps_ref[n * steps + t] for n in range(states))
        terms = [h[n] * maps_ref[(states + n) * steps + t] for n in range(states)]
        while len(terms) > 1:
            terms = [a + b for a, b in zip(terms[::2], terms[1::2])]
        rows[t] = terms[0]
        return h

    lax.fori_loop(0, steps, body, h, unroll=2)
    for j in range(8):
        at = slice(j * lanes, (j + 1) * lanes)
        gate = total([r[:, at] for r in gate_refs]) * scale_ref[...]
        out_ref[:, at] = ((rows[:, j, :] + skip_ref[:, at] * mixed_ref[:, at]) * silu(gate)).astype(BF)


def local_state(maps, low, weight, bias, mixed, rate):
    states, _, lanes = rate.shape
    steps = low.shape[1]
    return pl.pallas_call(
        state_kernel,
        out_shape=[jax.ShapeDtypeStruct((steps, 8, lanes), F32)] * 2
        + [jax.ShapeDtypeStruct((states + 2, 8, lanes), BF)],
        in_specs=[pl.BlockSpec(memory_space=pltpu.SMEM)]
        + [pl.BlockSpec(memory_space=pltpu.VMEM)] * 5,
        out_specs=[pl.BlockSpec(memory_space=pltpu.VMEM)] * 3,
        compiler_params=pltpu.CompilerParams(vmem_limit_bytes=16 * 1024 * 1024),
        name="local_state",
    )(maps, low, weight, bias.reshape(1, -1), mixed, rate)


def full_scan(place, maps, step, drive, rate, same, other, mixed, skip, scale, gates):
    return pl.pallas_call(
        scan_kernel,
        out_shape=jax.ShapeDtypeStruct(mixed.shape, BF),
        in_specs=[pl.BlockSpec(memory_space=pltpu.SMEM)] * 2 + [pl.BlockSpec(memory_space=pltpu.VMEM)] * 12,
        out_specs=pl.BlockSpec(memory_space=pltpu.VMEM),
        scratch_shapes=[pltpu.VMEM(step.shape, F32)],
        compiler_params=pltpu.CompilerParams(vmem_limit_bytes=16 * 1024 * 1024),
        name="full_scan",
    )(place, maps, step, drive, rate, same, other, mixed, skip.reshape(1, -1), scale, *gates)


def input_kernel(place_ref, inverse_ref, *refs):
    blocks, (near, far), outs, rows = refs[:4], refs[4:6], refs[6:10], refs[10]
    x, core, z = (place_ref[i] for i in range(3))
    ext = blocks[0].shape[0]
    main = ext - HALO
    half = near.shape[0]
    chunks = []
    for k in range(4):
        rows[k * ext : k * ext + main] = blocks[k][:main]
        before = jnp.where(lax.rem(z - k + 4, 4) == 0, 0.0, blocks[(k + 1) % 4][main:].astype(F32))
        halo = jnp.where(core == 1, blocks[k][main:].astype(F32), before)
        rows[k * ext + main : (k + 1) * ext] = halo.astype(BF)
        chunks.append(lax.rem(z - x - k + 8, 4))
    tile = 256
    for n in range(near.shape[1] // tile):
        at = slice(n * tile, (n + 1) * tile)
        out = jnp.dot(rows[:, :half], near[:, at], preferred_element_type=F32)
        out = out + jnp.dot(rows[:, half:], far[:, at], preferred_element_type=F32)
        for k in range(4):
            top, low = out[k * ext : k * ext + main].astype(BF), out[k * ext + main : (k + 1) * ext]
            if n == 0:
                raw = rows[k * ext : (k + 1) * ext].astype(F32) * inverse_ref[...]
                square = jnp.broadcast_to(jnp.sum(raw * raw, axis=1, keepdims=True), (ext, main))
                last = jnp.concatenate([square[main:], jnp.zeros((main - HALO, main), F32)], axis=0)
                row = jnp.concatenate([square[:main].T[:HALO], last.T[:HALO]], axis=1)
                high = row.astype(BF).astype(F32)
                which = lax.broadcasted_iota(jnp.int32, low.shape, 0)
                low = jnp.where(which == 0, high, jnp.where(which == 1, row - high, low))
            low = low.astype(BF)
            for m in range(4):

                @pl.when(chunks[k] == m)
                def _():
                    outs[m][:main, at] = top
                    outs[m][main:, at] = low


def input_product(place, inverse, blocks, near, far):
    ext, wide = blocks[0].shape
    return pl.pallas_call(
        input_kernel,
        out_shape=[jax.ShapeDtypeStruct((ext, near.shape[1]), BF)] * 4,
        in_specs=[pl.BlockSpec(memory_space=pltpu.SMEM)] + [pl.BlockSpec(memory_space=pltpu.VMEM)] * 7,
        out_specs=[pl.BlockSpec(memory_space=pltpu.VMEM)] * 4,
        scratch_shapes=[pltpu.VMEM((4 * ext, wide), BF)],
        compiler_params=pltpu.CompilerParams(vmem_limit_bytes=16 * 1024 * 1024),
        name="input_product",
    )(place, inverse.reshape(1, -1), *blocks, near, far)


def gate_kernel(place_ref, after_ref, *refs):
    blocks, (near, far), outs, rows = refs[:4], refs[4:6], refs[6:10], refs[10]
    x, z = place_ref[0], place_ref[2]
    main, half = outs[0].shape[0], near.shape[0]
    for k in range(4):
        rows[k * main : (k + 1) * main] = blocks[k][:main]
    tile = 256
    for n in range(near.shape[1] // tile):
        at = slice(n * tile, (n + 1) * tile)
        out = jnp.dot(rows[:, :half], near[:, at], preferred_element_type=F32)
        out = (out + jnp.dot(rows[:, half:], far[:, at], preferred_element_type=F32)).astype(BF)
        for k in range(4):
            chunk = lax.rem(z - x - k + 8, 4)
            for m in range(4):

                @pl.when(chunk == m)
                def _():
                    outs[m][:, at] = out[k * main : (k + 1) * main]


def gate_product(place, after, blocks, near, far):
    ext, wide = blocks[0].shape
    main = ext - HALO
    return pl.pallas_call(
        gate_kernel,
        out_shape=[jax.ShapeDtypeStruct((main, near.shape[1]), BF)] * 4,
        in_specs=[pl.BlockSpec(memory_space=pltpu.SMEM), pl.BlockSpec(memory_space=pl.ANY)]
        + [pl.BlockSpec(memory_space=pltpu.VMEM)] * 6,
        out_specs=[pl.BlockSpec(memory_space=pltpu.VMEM)] * 4,
        scratch_shapes=[pltpu.VMEM((4 * main, wide), BF)],
        compiler_params=pltpu.CompilerParams(vmem_limit_bytes=16 * 1024 * 1024),
        cost_estimate=pl.CostEstimate(flops=8 * main * wide * near.shape[1], bytes_accessed=6 * 2**20, transcendentals=0),
        name="gate_product",
    )(place, after, *blocks, near, far)


def sum_kernel(*refs):
    refs[-1][...] = total([r[...] for r in refs[:4]]).astype(BF)


def sum_after(blocks, after):
    return pl.pallas_call(
        sum_kernel,
        out_shape=jax.ShapeDtypeStruct(blocks[0].shape, BF),
        in_specs=[pl.BlockSpec(memory_space=pltpu.VMEM)] * 4 + [pl.BlockSpec(memory_space=pl.ANY)] * len(after),
        out_specs=pl.BlockSpec(memory_space=pltpu.VMEM),
        name="sum_after",
    )(*blocks, *after)


def beside_kernel(*refs):
    for k in range(4):
        refs[5][k] = total([r[k] for r in refs[:4]]).astype(BF)
    refs[6][...] = refs[4][...]


def sum_beside(blocks, rows):
    return pl.pallas_call(
        beside_kernel,
        out_shape=[jax.ShapeDtypeStruct(v.shape, BF) for v in (blocks[0], rows)],
        in_specs=[pl.BlockSpec(memory_space=pltpu.VMEM)] * 5,
        out_specs=[pl.BlockSpec(memory_space=pltpu.VMEM)] * 2,
        name="sum_beside",
    )(*blocks, rows)


def stack_kernel(*refs):
    for k in range(4):
        refs[8][k] = refs[k][...]
        refs[9][k] = refs[4 + k][...]


def stack_pair(first, second):
    return pl.pallas_call(
        stack_kernel,
        out_shape=[jax.ShapeDtypeStruct((4,) + v[0].shape, BF) for v in (first, second)],
        in_specs=[pl.BlockSpec(memory_space=pltpu.VMEM)] * 8,
        out_specs=[pl.BlockSpec(memory_space=pltpu.VMEM)] * 2,
        name="stack_pair",
    )(*first, *second)


def scatter_sum(blocks, axis, sign):
    return total([blocks[0]] + [shift(blocks[k], axis, sign * k % 4) for k in range(1, 4)])


def load_kernel(*refs):
    sources, targets, sem = refs[:3], refs[-4:-1], refs[-1]
    copies = [pltpu.make_async_copy(s, t, sem.at[n]) for n, (s, t) in enumerate(zip(sources, targets))]
    for copy in copies:
        copy.start()
    for copy in copies:
        copy.wait()


def load_weights(weights, after):
    return pl.pallas_call(
        load_kernel,
        out_shape=[jax.ShapeDtypeStruct(w.shape, w.dtype) for w in weights],
        in_specs=[pl.BlockSpec(memory_space=pl.ANY)] * (3 + len(after)),
        out_specs=[pl.BlockSpec(memory_space=pltpu.VMEM)] * 3,
        scratch_shapes=[pltpu.SemaphoreType.DMA((3,))],
        compiler_params=pltpu.CompilerParams(vmem_limit_bytes=24 * 1024 * 1024),
        cost_estimate=pl.CostEstimate(flops=0, bytes_accessed=2 * sum(w.size * 2 for w in weights), transcendentals=0),
        name="load_weights",
    )(*weights, *after)


def expert_kernel(place_ref, gain_ref, *refs):
    first, second, (gate_ref, up_ref, down_ref) = refs[:4], refs[4:8], refs[8:11]
    first_out, second_out, (batch, active) = refs[11:15], refs[15:19], refs[19:]
    _, count, wide = first[0].shape
    share = wide // 4
    width = batch.shape[1]
    x, z, y = place_ref[0], place_ref[2], place_ref[3]

    def column(i, j):
        return pl.multiple_of(lax.rem(x - i + 4, 4) * wide + lax.rem(y - j + 4, 4) * share, share)

    for half, source in enumerate((first, second)):
        for k in range(4):
            blocks = [(source[k][j] if half == 0 else source[j][k]).astype(F32) for j in range(4)]
            square = sum(jnp.sum(b * b, axis=1, keepdims=True) for b in blocks)
            scale = lax.rsqrt(square / width + EPS)
            top = pl.ds(pl.multiple_of((half * 4 + lax.rem(z - k - x + 8, 4)) * count, 16), count)
            for j in range(4):
                for i in range(4):
                    at = pl.ds(column(i, j), share)
                    piece = blocks[j][:, i * share : (i + 1) * share] * scale * gain_ref[:, at]
                    batch[top, at] = piece.astype(BF)
    for number in range(active.shape[1] // share):
        at = slice(number * share, (number + 1) * share)
        gate = jnp.dot(batch[...], gate_ref[:, at], preferred_element_type=F32)
        up = jnp.dot(batch[...], up_ref[:, at], preferred_element_type=F32)
        active[:, at] = (silu(gate) * up).astype(BF)
    for k in range(4):
        for j in range(4):
            column_out = lax.rem(z - k + 4, 4) * wide + lax.rem(y - j + 4, 4) * share
            at = pl.ds(pl.multiple_of(column_out, share), share)
            out = jnp.dot(active[...], down_ref[:, at], preferred_element_type=F32).astype(BF)
            first_out[k][j] = out[: 4 * count]
            second_out[j][k] = out[4 * count :]


def expert_block(place, gain, first, second, w_gate, w_up, w_down):
    width, hidden = w_gate.shape
    _, count, wide = first[0].shape
    out = pl.pallas_call(
        expert_kernel,
        out_shape=[jax.ShapeDtypeStruct((4, 4 * count, wide // 4), BF)] * 8,
        in_specs=[pl.BlockSpec(memory_space=pltpu.SMEM)] + [pl.BlockSpec(memory_space=pltpu.VMEM)] * 12,
        out_specs=[pl.BlockSpec(memory_space=pltpu.VMEM)] * 8,
        scratch_shapes=[pltpu.VMEM((8 * count, width), BF), pltpu.VMEM((8 * count, hidden), BF)],
        compiler_params=pltpu.CompilerParams(vmem_limit_bytes=12 * 1024 * 1024),
        cost_estimate=pl.CostEstimate(
            flops=48 * count * width * hidden, bytes_accessed=6 * width * hidden, transcendentals=8 * count * hidden
        ),
        name="expert_block",
    )(place, gain.reshape(1, -1), *first, *second, w_gate, w_up, w_down)
    return out[:4], out[4:]


def shards(
    tokens,
    norm_gain,
    in_x,
    in_z,
    conv_weight,
    conv_bias,
    xproj_weight,
    dt_weight,
    dt_bias,
    a_log,
    skip_d,
    out_weight,
    moe_gain,
    expert_ids,
    route_gates,
    w_gate,
    w_up,
    w_down,
):
    x, core, z, y = (lax.axis_index(a) for a in ("x", "core", "z", "y"))
    block_rows, col_share = tokens.shape
    width = norm_gain.shape[0]
    channels = in_x.shape[1]
    lanes = channels // 8
    rank = dt_weight.shape[0]
    states = a_log.shape[1]
    swap_cores = [(0, 1), (1, 0)]

    place = jnp.stack([x, core, z, y]).astype(jnp.int32)

    ids_rows = jnp.pad(expert_ids.T.astype(BF), ((0, HALO - expert_ids.shape[1]), (0, col_share - block_rows)))
    swapped = swap_xz(jnp.concatenate([tokens, ids_rows], axis=0))
    own = swapped[:block_rows]
    tail = lax.ppermute(own[block_rows - HALO :], "core", swap_cores)
    gains = lax.dynamic_slice_in_dim(norm_gain, x * 4 * col_share, 4 * col_share).reshape(4, col_share)
    gained = (jnp.concatenate([own, tail], axis=0).astype(F32) * pick(gains, y)).astype(BF)

    order = [(2 * core + i) % 4 for i in range(4)]
    parts = jnp.stack(gather_rel(gained, "y"))
    wide = jnp.concatenate([pick(parts, (y - o + 4) % 4) for o in order], axis=1)
    blocks = gather_rel(wide, "z")
    far_x = lax.ppermute(in_x, "core", swap_cores)
    far_z = lax.ppermute(in_z, "core", swap_cores)
    inverse = 1.0 / jnp.concatenate([pick(gains, o) for o in order])
    part_u = input_product(place, inverse, blocks, in_x, far_x)
    sum_u = scatter_sum(part_u, "x", 1)
    mean_sq = (sum_u[block_rows] + sum_u[block_rows + 1]) / width
    scale = lax.rsqrt(mean_sq[: block_rows + HALO] + EPS)[:, None]
    inner_u = sum_u * scale

    taps = conv_weight.shape[0]
    inner_u = jnp.concatenate([inner_u[block_rows + HALO - (taps - 1) :], inner_u[:block_rows]], axis=0)
    conv_sum = conv_bias + jnp.zeros((block_rows, channels), F32)
    for offset in range(taps):
        conv_sum = conv_sum + conv_weight[offset] * inner_u[offset : offset + block_rows]
    mixed_in = silu(conv_sum)

    part_p = lax.dot_general(
        xproj_weight, mixed_in.astype(BF), (((0,), (1,)), ((), ())), preferred_element_type=F32
    ).astype(BF)
    gate_raw = gate_product(place, part_u[0], blocks, in_z, far_z)
    gate_parts = [gate_raw[0]] + [shift(gate_raw[d], "x", d) for d in range(1, 4)]
    projected = sum_after(gather_rel(part_p, "y"), gate_parts[1:])
    projected = total(gather_rel(projected, "z")).astype(BF)

    dt_low = projected[:rank]
    maps = projected[rank:].astype(F32).reshape(-1)
    rate = (-jnp.exp(a_log) * LOG2E).T.reshape(states, 8, lanes)
    step, drive, ends = local_state(maps, dt_low, dt_weight, dt_bias, mixed_in, rate)
    same = jnp.stack(gather_rel(ends, "x"))
    other = lax.ppermute(same, "core", swap_cores)
    gated = full_scan(
        place, maps, step, drive, rate, same, other, mixed_in, skip_d, scale[:block_rows], gate_parts
    )

    far_out = lax.ppermute(out_weight, "core", swap_cores)
    out_both = jnp.where(
        core == 0,
        jnp.concatenate([out_weight, far_out], axis=1),
        jnp.concatenate([far_out, out_weight], axis=1),
    )
    gated_rows = jnp.concatenate(gather_rel(gated, "x"), axis=0)
    part_o = jnp.dot(gated_rows, out_both, preferred_element_type=F32).astype(BF).reshape(4, block_rows, -1)
    sum_o = scatter_sum([pick(part_o, (x - z - d + 8) % 4) for d in range(4)], "z", 1).astype(BF)
    sum_o = sum_o.reshape(block_rows, 4, col_share).transpose(1, 0, 2)
    mixer = scatter_sum([pick(sum_o, (y + d) % 4) for d in range(4)], "y", 1)
    resid = (own.astype(F32) + mixer).astype(BF)

    top = expert_ids.shape[1]
    experts = lax.axis_size("x") * lax.axis_size("core")
    capacity = block_rows * top * 3 // (2 * experts)
    flat = jnp.arange(block_rows * top, dtype=jnp.int32)
    before = (flat[:, None] > flat[None, :]).astype(BF)

    def slots(ids):
        one_hot = ids[:, None] == jnp.arange(experts, dtype=jnp.int32)[None, :]
        earlier = jnp.dot(before, one_hot.astype(BF), preferred_element_type=F32)
        return ids * capacity + jnp.sum(jnp.where(one_hot, earlier, 0.0), axis=1).astype(jnp.int32)

    def cells(sign):
        named = jnp.stack([2 * ((x + sign * d + 4) % 4) + (core + c) % 2 for c in range(2) for d in range(4)])
        return (named[:, None] * capacity + jnp.arange(capacity, dtype=jnp.int32)[None, :]).reshape(1, -1)

    away_ids = swapped[block_rows : block_rows + top, :block_rows].astype(jnp.int32).reshape(-1)
    send = slots(away_ids)[:, None] == cells(1)
    send = (send[:block_rows] | send[block_rows:]).astype(BF)
    fetch = (slots(expert_ids.T.reshape(-1))[:, None] == cells(-1)).astype(BF)

    outgoing = lax.dot_general(send, resid, (((0,), (0,)), ((), ())), preferred_element_type=F32).astype(BF)
    outgoing = outgoing.reshape(2, 4, capacity, col_share)
    both = jnp.stack([outgoing[0], lax.ppermute(outgoing[1], "core", swap_cores)], axis=1)
    received = [both[0]] + [shift(both[d], "x", d) for d in range(1, 4)]
    halves = jnp.concatenate(received, axis=2)

    first, second = stack_pair(gather_rel(halves[0], "y"), gather_rel(halves[1], "z"))
    weights = load_weights([w_gate[0], w_up[0], w_down[0]], [first])
    first, second = gather_rel(first, "z"), gather_rel(second, "y")
    first, second = expert_block(place, moe_gain, first, second, *weights)
    first = scatter_sum(scatter_sum(first, "z", -1).astype(BF), "y", -1).astype(BF)
    second, resid = sum_beside([second[0]] + [shift(second[k], "y", 4 - k) for k in range(1, 4)], resid)
    resid_home = swap_xz(resid)
    second = scatter_sum(second, "z", -1).astype(BF)
    back = jnp.stack([first.reshape(4, capacity, col_share), second.reshape(4, capacity, col_share)], axis=1)
    back = [back[0]] + [shift(back[r], "x", r) for r in range(1, 4)]
    far_back = lax.ppermute(jnp.stack([b[1] for b in back]), "core", swap_cores)
    returned = jnp.concatenate([b[0] for b in back] + [far_back.reshape(4 * capacity, col_share)], axis=0)
    picked = jnp.dot(fetch, returned, preferred_element_type=F32)
    moe = picked[:block_rows] * route_gates[:, :1] + picked[block_rows:] * route_gates[:, 1:]
    return (resid_home.astype(F32) + moe).astype(BF)


def solution(mesh):
    fine = Mesh(mesh.devices.reshape(4, 2, 4, 4), ("x", "core", "z", "y"))
    section, tp = ("x", "core"), ("z", "y")
    placed = (
        P(section, tp),
        P(),
        P(section, tp),
        P(section, tp),
        P(None, tp),
        P(tp),
        P(tp, None),
        P(None, tp),
        P(tp),
        P(tp, None),
        P(tp),
        P(tp, section),
        P(),
        P(section, None),
        P(section, None),
        P(section, None, tp),
        P(section, None, tp),
        P(section, tp, None),
    )
    return jax.shard_map(
        shards, mesh=fine, in_specs=placed, out_specs=P(section, tp), check_vma=False
    )
```
